256 devices in a mesh: plane: 8 (over z), mode: 32 (over y, x, core).
Axes of the slice: x: 4, y: 4, z: 8, core: 2. Of those that a mesh axis runs over, the one named last changes fastest.
Arguments:
- velocity: float32 [3, 512, 49, 1024], P(None, 'mode', None, 'plane'), may hold values from -8 to 8
- metric_terms: float32 [4, 49, 1024], P(None, None, 'plane'), may hold values from -1.75 to 1.75
- lift_scale: float32 [2, 4, 7, 1024], P(None, None, None, 'plane'), may hold values from -6 to 6
- neighbour: int32 [4, 1024], P(None, 'plane'), may hold values from -1 to 1023, as said below
- neighbour_side: int32 [4, 1024], P(None, 'plane'), may hold values from 0 to 3, as said below
- orientation: int32 [4, 1024], P(None, 'plane'), may hold values from 0 to 1, as said below
Outputs:
- advection: float32 [3, 512, 49, 1024], P(None, 'mode', None, 'plane')
The draws below stay inside these ranges and needn't reach their ends.
Inputs may be any that keep to these rules, and one draw needn't show every extreme that they name: neighbour[s, e] is the element across side s of element e, or -1 on the domain's boundary; it lies in the same partition of 128 elements as e or in an adjacent one, and the relation is symmetric: neighbour[neighbour_side[s, e], neighbour[s, e]] = e. Partitions p and p + 1 share 20 or 21 sides, partitions 0 and 1 exactly 21. 0 where neighbour is -1; otherwise neighbour_side[neighbour_side[s, e], neighbour[s, e]] = s. `orientation`: 0 where neighbour is -1; the same value seen from both elements of a shared side.
All inputs are finite; a program needn't handle non-finite values.
Results may differ from the reference program's by a relative error of at most 0.000096.
Values sent between devices are 32-bit elements; how exact they have to be, the bound alone decides.
A program may use at most 128 MiB of HBM per device.

```python
import math
import jax
import jax.numpy as jnp
import numpy as np
from jax import lax

NP = 7
NN = 49
NZ = 512
E_DEV = 128
GY = 20
ELEMS = 1024


def draw_velocity(key, part):
    coef_index = jnp.arange(NZ, dtype=jnp.int32)
    wavenumber = jnp.where(coef_index == 1, NZ // 2, coef_index // 2).astype(jnp.float32)
    envelope = 1.0 / (1.0 + wavenumber / 16.0)
    samples = jnp.clip(jax.random.normal(key, (3, NZ, NP * NP, ELEMS), jnp.float32), -6.0, 6.0)
    values = samples * envelope[None, :, None, None]
    mean_flow = jnp.where(coef_index == 0, 1.0, 0.0).astype(jnp.float32)
    return values.at[0].add(mean_flow[:, None, None])


def mesh_tables(key):
    grid_index = jnp.arange(ELEMS, dtype=jnp.int32)
    rotation_grid = jax.random.randint(jax.random.fold_in(key, 11), (ELEMS,), 0, 4).astype(jnp.int32)
    orders = jax.vmap(lambda subkey: jax.random.permutation(subkey, E_DEV))(jax.random.split(jax.random.fold_in(key, 12), ELEMS // E_DEV))
    slot_of_grid = grid_index // E_DEV * E_DEV + orders.reshape(-1).astype(jnp.int32)
    grid_of_slot = jnp.zeros((ELEMS,), jnp.int32).at[slot_of_grid].set(grid_index)
    row_of = grid_index % GY
    below = jnp.where(row_of > 0, grid_index - 1, -1)
    right_grid = jnp.where(grid_index + GY < ELEMS, grid_index + GY, -1)
    above = jnp.where((row_of < GY - 1) & (grid_index + 1 < ELEMS), grid_index + 1, -1)
    left_grid = jnp.where(grid_index >= GY, grid_index - GY, -1)
    grid_across = jnp.stack([below, right_grid, above, left_grid]).astype(jnp.int32)
    side_index = jnp.arange(4, dtype=jnp.int32)[:, None]
    own_grid = jnp.broadcast_to(grid_of_slot[None, :], (4, ELEMS))
    direction = (side_index + rotation_grid[own_grid]) % 4
    other_grid = grid_across[direction, own_grid]
    exists = other_grid >= 0
    safe_grid = jnp.where(exists, other_grid, 0)
    neighbour = jnp.where(exists, slot_of_grid[safe_grid], -1).astype(jnp.int32)
    back_side = jnp.where(exists, (direction + 2 - rotation_grid[safe_grid]) % 4, 0).astype(jnp.int32)
    mine_reversed = (side_index >= 2).astype(jnp.int32)
    theirs_reversed = (back_side >= 2).astype(jnp.int32)
    orientation = jnp.where(exists, 1 - (mine_reversed ^ theirs_reversed), 0).astype(jnp.int32)
    return (neighbour, back_side, orientation)


def draw_neighbour(key, part):
    return mesh_tables(key)[0]


def draw_neighbour_side(key, part):
    return mesh_tables(key)[1]


def draw_orientation(key, part):
    return mesh_tables(key)[2]


def levels(rng, extent, cuts, low, top_value):
    loudness, own = 1.0, jax.random.fold_in(rng, 6)
    for axis_at, parts in cuts:
        steps = jnp.exp(jax.random.uniform(jax.random.fold_in(own, axis_at), (parts,), jnp.float32, low / len(cuts), top_value / len(cuts)))
        loudness = loudness * jnp.repeat(steps, extent[axis_at] // parts).reshape([-1 if axis == axis_at else 1 for axis in range(len(extent))])
    return loudness


def centred(own_key, extent, scale, reach, cuts=(), kind=jnp.bfloat16):
    gain = levels(own_key, extent, cuts, -0.22, 0.18) if cuts else 1.0
    drawn = jax.random.normal(own_key, extent, jnp.float32) * scale * gain
    return jnp.minimum(jnp.maximum(drawn, -reach), reach).astype(kind)


def setup_inputs(seed: int = 0) -> dict:
    key_list = jax.random.split(jax.random.key(seed), 7)
    return {
        "velocity": draw_velocity(jax.random.fold_in(key_list[6], 71), 0),
        "metric_terms": centred(key_list[1], (4, NN, ELEMS), 0.3, 1.75, ((2, 8),), jnp.float32),
        "lift_scale": centred(key_list[2], (2, 4, NP, ELEMS), 1.0, 6.0, ((3, 8),), jnp.float32),
        "neighbour": draw_neighbour(jax.random.fold_in(key_list[6], 71), 0),
        "neighbour_side": draw_neighbour_side(jax.random.fold_in(key_list[6], 71), 0),
        "orientation": draw_orientation(jax.random.fold_in(key_list[6], 71), 0),
    }


GLL_POINTS = (-1.0, -0.830223896278567, -0.468848793470714, 0.0, 0.468848793470714, 0.830223896278567, 1.0)
SPAN_WAVENUMBER = 0.25
EXACT = lax.Precision.HIGHEST


def derivative_matrix():
    points = np.array(GLL_POINTS)
    identity = np.eye(points.shape[0])
    differ = points[:, None] - points[None, :]
    offdiag = differ + identity
    weights = 1.0 / np.prod(offdiag, axis=1)
    matrix = (weights[None, :] / weights[:, None]) / offdiag
    matrix = matrix * (1.0 - identity)
    matrix = matrix - identity * matrix.sum(axis=1)[:, None]
    return jnp.asarray(matrix, dtype=jnp.float32)


def trace_selector():
    last_node = NP - 1
    selector = np.zeros((4 * NP, NP * NP))
    for position in range(NP):
        selector[position, position] = 1.0
        selector[NP + position, position * NP + last_node] = 1.0
        selector[2 * NP + position, last_node * NP + position] = 1.0
        selector[3 * NP + position, position * NP] = 1.0
    return jnp.asarray(selector, dtype=jnp.float32)


def spectral_tables(planes):
    coef_index = jnp.arange(planes, dtype=jnp.int32)
    wavenumber = jnp.where(coef_index == 1, planes // 2, coef_index // 2)
    phase = (wavenumber[:, None] * coef_index[None, :]) % planes
    phase_angle = phase.astype(jnp.float32) * (2.0 * math.pi / planes)
    sine_row = (coef_index % 2 == 1) & (coef_index > 1)
    inverse = jnp.where(sine_row[:, None], jnp.sin(phase_angle), jnp.cos(phase_angle))
    weighting = jnp.where(coef_index < 2, jnp.float32(1.0), jnp.float32(2.0)) / planes
    forward = inverse.T * weighting[None, :]
    return inverse, forward


def spanwise_gradient(spectral, first_index):
    how_many = spectral.shape[1]
    coef_index = first_index + jnp.arange(how_many, dtype=jnp.int32)
    wavenumber = jnp.where(coef_index < 2, 0, coef_index // 2).astype(jnp.float32) * SPAN_WAVENUMBER
    paired = spectral.reshape((spectral.shape[0], how_many // 2, 2) + spectral.shape[2:])
    swapped = jnp.stack([paired[:, :, 1], -paired[:, :, 0]], axis=2).reshape(spectral.shape)
    return swapped * wavenumber[None, :, None, None]


def spectral_derivs(spectral, matrix):
    in_shape = spectral.shape
    nodal = spectral.reshape(in_shape[:2] + (NP, NP) + in_shape[3:])
    along_xi = jnp.einsum('ab,fcjbe->fcjae', matrix, nodal, precision=EXACT)
    along_eta = jnp.einsum('ab,fcbie->fcaie', matrix, nodal, precision=EXACT)
    return along_xi.reshape(in_shape), along_eta.reshape(in_shape)


def reference(velocity, metric_terms, lift_scale, neighbour, neighbour_side, orientation):
    matrix = derivative_matrix()
    selector = trace_selector()
    inverse, forward = spectral_tables(NZ)
    exists = neighbour >= 0
    safe_slot = jnp.where(exists, neighbour, 0).astype(jnp.int32)
    position = jnp.arange(NP, dtype=jnp.int32)
    source_pos = jnp.where(orientation[:, None, :] == 1, NP - 1 - position[None, :, None], position[None, :, None])
    source_row = (neighbour_side[:, None, :] * NP + source_pos).reshape(4 * NP, ELEMS).astype(jnp.int32)
    source_col = jnp.broadcast_to(safe_slot[:, None, :], (4, NP, ELEMS)).reshape(4 * NP, ELEMS)
    edge_live = jnp.broadcast_to(exists[:, None, :], (4, NP, ELEMS)).reshape(4 * NP, ELEMS)

    def field_jump(component):
        traces = jnp.einsum('tn,cne->cte', selector, component, precision=EXACT)
        across = traces[:, source_row, source_col]
        return jnp.where(edge_live[None], 0.5 * (across - traces), jnp.zeros_like(traces))

    edge_jump = lax.map(field_jump, velocity)
    blocks = ELEMS // E_DEV

    def split_blocks(array):
        return jnp.moveaxis(array.reshape(array.shape[:-1] + (blocks, E_DEV)), -2, 0)

    lift_flat = lift_scale.reshape(2, 4 * NP, ELEMS)

    def block_advection(pieces):
        spectral, jumps, metric, lifts = pieces
        along_xi, along_eta = spectral_derivs(spectral, matrix)
        lifted_x = jnp.einsum('tn,fcte->fcne', selector, jumps * lifts[0], precision=EXACT)
        lifted_y = jnp.einsum('tn,fcte->fcne', selector, jumps * lifts[1], precision=EXACT)
        grad_x = metric[0] * along_xi + metric[2] * along_eta + lifted_x
        grad_y = metric[1] * along_xi + metric[3] * along_eta + lifted_y
        grad_z = spanwise_gradient(spectral, 0)
        stacked = jnp.concatenate([spectral, grad_x, grad_y, grad_z], axis=0)
        physical = jnp.einsum('cz,fcne->fnez', inverse, stacked, precision=EXACT)
        product = physical[0][None] * physical[3:6] + physical[1][None] * physical[6:9] + physical[2][None] * physical[9:12]
        return jnp.einsum('zc,fnez->fcne', forward, product, precision=EXACT)

    result = lax.map(block_advection, (split_blocks(velocity), split_blocks(edge_jump), split_blocks(metric_terms), split_blocks(lift_flat)))
    return jnp.moveaxis(result, 0, -2).reshape(3, NZ, NP * NP, ELEMS)
```

```python
import jax
import jax.numpy as jnp
import ml_dtypes
import numpy as np
from jax import lax
from jax.experimental import pallas as pl
from jax.experimental.pallas import tpu as pltpu
from jax.sharding import PartitionSpec as P

MESH = pl.DeviceIdType.MESH
F32 = jnp.float32
BF16 = jnp.bfloat16

NP = 7
NN = 49
NZ = 512
MODES = 32
PLANES = 8
LOCAL = 16
ELEMS = 128
SPAN_WAVENUMBER = 0.25
VEL_GROUPS = 5
GROUPS = 8

GLL_POINTS = (
    -1.0,
    -0.830223896278567,
    -0.468848793470714,
    0.0,
    0.468848793470714,
    0.830223896278567,
    1.0,
)

PIECES = (
    (0, 0, 0, 32),
    (1, 0, 32, 17),
    (1, 17, 130, 15),
    (2, 0, 49, 32),
    (3, 0, 81, 17),
    (3, 17, 145, 2),
    (4, 0, 98, 32),
)


def derivative_matrix():
    points = np.array(GLL_POINTS)
    identity = np.eye(NP)
    offdiag = points[:, None] - points[None, :] + identity
    weights = 1.0 / np.prod(offdiag, axis=1)
    matrix = weights[None, :] / weights[:, None] / offdiag
    matrix = matrix * (1.0 - identity)
    return matrix - identity * matrix.sum(axis=1)[:, None]


def split_np(table):
    table = table.astype(np.float32)
    high = table.astype(ml_dtypes.bfloat16)
    low = (table - high.astype(np.float32)).astype(ml_dtypes.bfloat16)
    return high, low


def side_node(side, position):
    return (position, position * NP + NP - 1, (NP - 1) * NP + position, position * NP)[side]


def tables():
    index = np.arange(NZ)
    wave = np.where(index == 1, NZ // 2, index // 2)
    phase = (wave[:, None] * index[None, :] % NZ) * (2.0 * np.pi / NZ)
    sine_row = ((index % 2 == 1) & (index > 1))[:, None]
    inverse = np.where(sine_row, np.sin(phase), np.cos(phase))
    slope = np.where(index < 2, 0.0, wave)[:, None] * SPAN_WAVENUMBER
    slope = slope * np.where(sine_row, np.cos(phase), -np.sin(phase))
    weighting = np.where(index < 2, 1.0, 2.0) / NZ
    high, low = split_np(np.concatenate([inverse.T, slope.T], axis=0))
    backward = np.concatenate([high, low, high], axis=1)
    high, low = split_np(inverse * weighting[:, None])
    forward = np.concatenate([high, low, high], axis=1)
    matrix = derivative_matrix()
    derive = np.zeros((256, 512))
    for j in range(NP):
        for i in range(NP):
            for b in range(NP):
                for e in range(4):
                    derive[4 * (j * NP + b) + e, 4 * (j * NP + i) + e] = matrix[i, b]
                    derive[4 * (b * NP + i) + e, 256 + 4 * (j * NP + i) + e] = matrix[j, b]
    high, low = split_np(derive)
    derive = np.concatenate([high, high, low], axis=0)
    place = np.zeros((128, 512))
    for side in range(4):
        for position in range(NP):
            for e in range(4):
                column = 4 * side_node(side, position) + e
                place[4 * (side * NP + position) + e, 256 * (side % 2) + column] = 1.0
    place = place.astype(ml_dtypes.bfloat16)
    return backward, forward, derive, np.concatenate([place, place], axis=0)


def halves(value):
    high = value.astype(BF16)
    return high, (value - high.astype(F32)).astype(BF16)


def lane_swap(load, store):
    lane = lax.broadcasted_iota(jnp.int32, (8, 128), 1)
    tiles = [load(p) for p in range(32)]
    for bit in range(5):
        step = 4 << bit
        mask = (lane & step) != 0
        for p in range(32):
            if p >> bit & 1:
                continue
            q = p | 1 << bit
            a, b = tiles[p], tiles[q]
            tiles[p] = jnp.where(mask, pltpu.roll(b, step, 1), a)
            tiles[q] = jnp.where(mask, b, pltpu.roll(a, 128 - step, 1))
    for d in range(32):
        store(d, tiles[d])


def matmul(a, b):
    return jnp.dot(a, b, preferred_element_type=F32)


def matmul_nt(a, b):
    return lax.dot_general(a, b, (((1,), (1,)), ((), ())), preferred_element_type=F32)


def exact(a, b):
    return jnp.dot(a, b, precision=lax.Precision.HIGHEST, preferred_element_type=F32)


def main_kernel(
    v_hbm,
    metric_hbm,
    lift_hbm,
    nb_hbm,
    ns_hbm,
    or_hbm,
    inv_hbm,
    fwd_hbm,
    der_hbm,
    place_hbm,
    back,
    vn,
    vs,
    sb,
    rx,
    sb2,
    inv,
    fwd,
    der,
    place,
    met,
    lif,
    nbv,
    nsv,
    orv,
    lmat,
    kmat,
    oh,
    sel,
    oht,
    up_out,
    dn_out,
    up_in,
    dn_in,
    rows,
    xr,
    pv,
    dlhs,
    dxe,
    base,
    uu,
    xa,
    la,
    xp,
    tail,
    load_sem,
    in_sem,
    send_sem,
    recv_sem,
    send2_sem,
    recv2_sem,
    halo_send,
    halo_recv,
):
    me = lax.axis_index("mode")
    part = lax.axis_index("plane")
    above = lax.rem(part + 1, PLANES)
    below = lax.rem(part + PLANES - 1, PLANES)

    nbv[...] = jnp.full((8, 128), -1, jnp.int32)
    nsv[...] = jnp.zeros((8, 128), jnp.int32)
    orv[...] = jnp.zeros((8, 128), jnp.int32)
    met[...] = jnp.zeros_like(met)
    lif[...] = jnp.zeros_like(lif)
    loads = []
    for k, (group, slot, row, count) in enumerate(PIECES):
        copy = pltpu.make_async_copy(
            v_hbm.at[pl.ds(row, count)], vs.at[group, pl.ds(slot, count)], load_sem.at[k]
        )
        copy.start()
        loads.append((group, copy))
    others = []
    for k, (src, dst) in enumerate(
        (
            (v_hbm, vn),
            (nb_hbm, nbv.at[pl.ds(0, 4)]),
            (ns_hbm, nsv.at[pl.ds(0, 4)]),
            (or_hbm, orv.at[pl.ds(0, 4)]),
            (metric_hbm, met.at[:, pl.ds(0, 4)]),
            (lift_hbm, lif.at[:, pl.ds(0, 4)]),
            (inv_hbm, inv),
            (der_hbm, der),
            (place_hbm, place),
            (fwd_hbm, fwd),
        )
    ):
        copy = pltpu.make_async_copy(src, dst, in_sem.at[k])
        copy.start()
        others.append(copy)

    barrier = pltpu.get_barrier_semaphore()

    @pl.loop(1, MODES)
    def _(k):
        pl.semaphore_signal(
            barrier, inc=1, device_id={"mode": lax.rem(me + k, MODES)}, device_id_type=MESH
        )

    for other in (above, below):
        pl.semaphore_signal(barrier, inc=1, device_id={"plane": other}, device_id_type=MESH)

    vs[3, pl.ds(19, 13)] = jnp.zeros((13, LOCAL, 128), F32)
    for comp in range(3):
        vs[VEL_GROUPS + comp, pl.ds(28, 4)] = jnp.zeros((4, LOCAL, 128), F32)

    def scatter(group):
        @pl.loop(0, 2)
        def _(half):
            rows8 = pl.ds(pl.multiple_of(half * 8, 8), 8)

            def store(d, tile):
                sb[group, d, rows8] = tile

            lane_swap(lambda p: vs[group, p, rows8], store)

    def send(group):
        mine = rx.at[group, pl.ds(pl.multiple_of(me * LOCAL, LOCAL), LOCAL)]
        pltpu.make_async_copy(sb.at[group, me], mine, recv_sem.at[group]).start()

        @pl.loop(1, MODES)
        def _(k):
            to = lax.rem(me + k, MODES)
            pltpu.make_async_remote_copy(
                src_ref=sb.at[group, to],
                dst_ref=mine,
                send_sem=send_sem.at[group],
                recv_sem=recv_sem.at[group],
                device_id={"mode": to},
                device_id_type=MESH,
            ).start()

    for group in range(VEL_GROUPS):
        for owner, copy in loads:
            if owner == group:
                copy.wait()
        scatter(group)
        if group == 0:
            pl.semaphore_wait(barrier, MODES + 1)
        send(group)

    for copy in others[:4]:
        copy.wait()
    nb = nbv[...]
    exists = nb >= 0
    owner = lax.shift_right_arithmetic(nb, 7)
    target = nsv[...] * ELEMS + (nb & (ELEMS - 1))
    own_key = jnp.where(exists & (owner == part), target, -1)
    is_up = exists & (owner == part + 1)
    is_dn = exists & (owner == part - 1)
    strict = (
        lax.broadcasted_iota(jnp.int32, (128, 128), 0)
        < lax.broadcasted_iota(jnp.int32, (128, 128), 1)
    ).astype(F32)
    ranks = []
    for border in (is_up, is_dn):
        flag = jnp.where(border, 1.0, 0.0)
        before = exact(flag, strict)
        totals = jnp.sum(flag, axis=1, keepdims=True)
        offset = jnp.zeros((1, 1), F32)
        out = []
        for side in range(4):
            out.append(before[side : side + 1] + offset)
            offset = offset + totals[side : side + 1]
        ranks.append(out)
    row128 = lax.broadcasted_iota(jnp.int32, (128, 128), 0).astype(F32)
    row512 = lax.broadcasted_iota(jnp.int32, (512, 128), 0)
    for side in range(4):
        lanes = pl.ds(side * 128, 128)
        one = slice(side, side + 1)
        slot = jnp.where(
            is_up[one], ranks[0][side], jnp.where(is_dn[one], 32.0 + ranks[1][side], -1.0)
        )
        sel[:, lanes] = jnp.where(row128 == slot, 1.0, 0.0).astype(BF16)
        oh[:, lanes] = jnp.where(row512 == own_key[one], 1.0, 0.0).astype(BF16)
        high, low = halves(jnp.broadcast_to((target[one] + 1).astype(F32), (16, 128)))
        kmat[pl.ds(0, 16), lanes] = high
        kmat[pl.ds(16, 16), lanes] = low
    turned = orv[...] == 1

    @pl.loop(0, 3)
    def _(comp):
        for position in range(NP):
            for side in range(4):
                straight = vn[comp * NN + side_node(side, position)]
                reverse = vn[comp * NN + side_node(side, NP - 1 - position)]
                value = jnp.where(turned[side : side + 1], reverse, straight)
                high, low = halves(value)
                lanes = pl.ds(side * 128, 128)
                lmat[comp, pl.ds(position * 16, 16), lanes] = high
                lmat[comp, pl.ds(112 + position * 16, 16), lanes] = low

    picked = []
    for comp in range(3):
        both = matmul_nt(lmat[comp], sel[...])
        picked.append(both[:112] + both[112:])
    both = matmul_nt(kmat[...], sel[...])
    keys = jnp.concatenate([both[:16] + both[16:], jnp.zeros((96, 128), F32)], axis=0)
    picked.append(keys)
    lane = lax.broadcasted_iota(jnp.int32, (112, 128), 1)
    for ref, shift in ((up_out, 0), (dn_out, 96)):
        packed = None
        for k in (3, 2, 1, 0):
            by = (32 * k + shift) % 128
            moved = pltpu.roll(picked[k], by, 1) if by else picked[k]
            packed = moved if packed is None else jnp.where(lane < 32 * k + 32, moved, packed)
        ref[...] = packed
    halo = []
    for k, (src, dst, to) in enumerate(((up_out, up_in, above), (dn_out, dn_in, below))):
        copy = pltpu.make_async_remote_copy(
            src_ref=src,
            dst_ref=dst,
            send_sem=halo_send.at[k],
            recv_sem=halo_recv.at[k],
            device_id={"plane": to},
            device_id_type=MESH,
        )
        copy.start()
        halo.append(copy)

    for copy in others[4:6]:
        copy.wait()
    fold = (
        lax.broadcasted_iota(jnp.int32, (128, 256), 0)
        == 4 * me + (lax.broadcasted_iota(jnp.int32, (128, 256), 1) & 3)
    ).astype(F32)
    spread = exact(met[...].reshape(NN * 8, 128), fold).reshape(NN, 8, 256)
    node3 = lax.shift_right_arithmetic(lax.broadcasted_iota(jnp.int32, (NN, 8, 256), 2), 2)
    here = node3 == lax.broadcasted_iota(jnp.int32, (NN, 8, 256), 0)
    metric_rows = jnp.sum(jnp.where(here, spread, 0.0), axis=0)
    rows[pl.ds(0, 4)] = metric_rows[:4]
    live = exact(jnp.where(exists, 0.5, 0.0), fold)
    spread = exact(lif[...].reshape(2 * NP * 8, 128), fold).reshape(2 * NP, 8, 256)
    node2 = lax.shift_right_arithmetic(lax.broadcasted_iota(jnp.int32, (8, 256), 1), 2)
    side2 = lax.broadcasted_iota(jnp.int32, (8, 256), 0)
    for axis in range(2):
        total = jnp.zeros((8, 256), F32)
        for position in range(NP):
            wanted = jnp.full((8, 256), -1, jnp.int32)
            for side in range(4):
                wanted = jnp.where(side2 == side, side_node(side, position), wanted)
            total = total + jnp.where(node2 == wanted, spread[axis * NP + position], 0.0)
        total = total * live
        rows[pl.ds(4 + axis, 1)] = total[0:1] + total[2:3]
        rows[pl.ds(6 + axis, 1)] = total[1:2] + total[3:4]

    for copy in halo:
        copy.wait_recv()
    lane1 = lax.broadcasted_iota(jnp.int32, (8, 128), 1)
    key_up = pltpu.roll(up_in[pl.ds(0, 8)], 32, 1)
    key_dn = pltpu.roll(dn_in[pl.ds(0, 8)], 64, 1)
    key = jnp.where(lane1 < 32, key_up, jnp.where(lane1 < 64, key_dn, 0.0))[0:1]
    oht[...] = jnp.where((row512 + 1).astype(F32) == key, 1.0, 0.0).astype(BF16)
    for comp in range(3):
        both = matmul(lmat[comp], oh[...])
        across = both[:112] + both[112:]
        from_up = pltpu.roll(up_in[...], (128 - 32 * comp) % 128, 1) if comp else up_in[...]
        from_dn = pltpu.roll(dn_in[...], (160 - 32 * comp) % 128, 1) if comp != 1 else dn_in[...]
        high, low = halves(jnp.where(lane < 32, from_up, jnp.where(lane < 64, from_dn, 0.0)))
        both = matmul_nt(jnp.concatenate([high, low], axis=0), oht[...])
        across = across + (both[:112] + both[112:])
        for side in range(4):
            for position in range(NP):
                vs[VEL_GROUPS + comp, side * NP + position] = across[
                    position * 16 : position * 16 + 16, side * 128 : side * 128 + 128
                ]
        scatter(VEL_GROUPS + comp)
        send(VEL_GROUPS + comp)

    def received(group):
        pltpu.make_async_copy(rx.at[group], rx.at[group], recv_sem.at[group]).wait()

    for copy in others[6:]:
        copy.wait()
    for group in range(VEL_GROUPS):
        received(group)
    lane64 = lax.broadcasted_iota(jnp.int32, (64, 128), 1)

    @pl.loop(0, 8)
    def _(block):
        at = pl.multiple_of(block * 64, 64)
        rows64 = pl.ds(at, 64)
        g1, g3 = rx[1, rows64], rx[3, rows64]
        last = jnp.where(lane64 < 60, pltpu.roll(g1, 60, 1), pltpu.roll(g3, 120, 1))
        pieces = ((rx[0, rows64], g1), (rx[2, rows64], g3), (rx[4, rows64], last))
        for comp in range(3):
            for k in range(2):
                high, low = halves(pieces[comp][k])
                lanes = pl.ds(k * 128, 128)
                xr[comp, rows64, lanes] = high
                xr[comp, pl.ds(at + 512, 64), lanes] = high
                xr[comp, pl.ds(at + 1024, 64), lanes] = low

    @pl.loop(0, 3)
    def _(comp):
        pv[comp] = matmul(inv[...], xr[comp])

    @pl.loop(0, 8)
    def _(block):
        rows64 = pl.ds(pl.multiple_of(block * 64, 64), 64)
        u, v = pv[0, rows64], pv[1, rows64]
        for k in range(4):
            first, second = ((0, 1), (2, 3), (4, 5), (6, 7))[k]
            uu[k, rows64] = u * rows[pl.ds(first, 1)] + v * rows[pl.ds(second, 1)]

    @pl.loop(0, 3)
    def _(comp):
        @pl.loop(0, 8)
        def _(block):
            rows64 = pl.ds(pl.multiple_of(block * 64, 64), 64)
            high, low = halves(pv[comp, rows64])
            dlhs[rows64, pl.ds(0, 256)] = high
            dlhs[rows64, pl.ds(256, 256)] = low
            dlhs[rows64, pl.ds(512, 256)] = high

        dxe[...] = matmul(dlhs[...], der[...])

        @pl.loop(0, 8)
        def _(block):
            at = pl.multiple_of(block * 64, 64)
            rows64 = pl.ds(at, 64)
            total = uu[0, rows64] * dxe[rows64, pl.ds(0, 256)]
            total = total + uu[1, rows64] * dxe[rows64, pl.ds(256, 256)]
            total = total + pv[2, rows64] * pv[comp, pl.ds(at + 512, 64)]
            base[comp, rows64] = total - (uu[2, rows64] + uu[3, rows64]) * pv[comp, rows64]

    def send_back(group):
        pltpu.make_async_copy(
            sb2.at[group, pl.ds(pl.multiple_of(me * LOCAL, LOCAL), LOCAL)],
            back.at[group, me],
            recv2_sem.at[group],
        ).start()

        @pl.loop(1, MODES)
        def _(k):
            to = lax.rem(me + k, MODES)
            pltpu.make_async_remote_copy(
                src_ref=sb2.at[group, pl.ds(pl.multiple_of(to * LOCAL, LOCAL), LOCAL)],
                dst_ref=back.at[group, me],
                send_sem=send2_sem.at[group],
                recv_sem=recv2_sem.at[group],
                device_id={"mode": to},
                device_id_type=MESH,
            ).start()

    @pl.loop(0, 3)
    def _(comp):
        received(VEL_GROUPS + comp)

        @pl.loop(0, 8)
        def _(block):
            at = pl.multiple_of(block * 64, 64)
            high, low = halves(rx[VEL_GROUPS + comp, pl.ds(at, 64)])
            xa[pl.ds(at, 64)] = high
            xa[pl.ds(at + 512, 64)] = high
            xa[pl.ds(at + 1024, 64)] = low

        high, low = halves(matmul(inv[pl.ds(0, 512)], xa[...]))
        la[:, pl.ds(0, 128)] = high
        la[:, pl.ds(128, 128)] = low
        dxe[...] = matmul(la[...], place[...])

        @pl.loop(0, 8)
        def _(block):
            at = pl.multiple_of(block * 64, 64)
            rows64 = pl.ds(at, 64)
            total = base[comp, rows64] + uu[2, rows64] * dxe[rows64, pl.ds(0, 256)]
            total = total + uu[3, rows64] * dxe[rows64, pl.ds(256, 256)]
            high, low = halves(total)
            xp[rows64] = high
            xp[pl.ds(at + 512, 64)] = high
            xp[pl.ds(at + 1024, 64)] = low

        result = matmul(fwd[...], xp[...])
        sb2[2 * comp] = result[:, :128]
        tail[comp] = result[:, 128:]
        send_back(2 * comp)

    @pl.loop(0, 8)
    def _(block):
        rows64 = pl.ds(pl.multiple_of(block * 64, 64), 64)
        last = tail[2, rows64]
        sb2[1, rows64] = jnp.where(lane64 < 68, tail[0, rows64], pltpu.roll(last, 68, 1))
        sb2[3, rows64] = jnp.where(lane64 < 68, tail[1, rows64], pltpu.roll(last, 8, 1))

    send_back(1)
    send_back(3)

    for copy in halo:
        copy.wait_send()
    for group in range(GROUPS):
        sent = sb.at[group, pl.ds(0, MODES - 1)]
        pltpu.make_async_copy(sent, sent, send_sem.at[group]).wait()
    for group in range(VEL_GROUPS):
        sent = sb2.at[group, pl.ds(0, (MODES - 1) * LOCAL)]
        pltpu.make_async_copy(sent, sent, send2_sem.at[group]).wait()
    for group in range(VEL_GROUPS):
        pltpu.make_async_copy(back.at[group], back.at[group], recv2_sem.at[group]).wait()


def last_kernel(back, out, blocks, done, in_sem, out_sem):
    copies = []
    for group in range(VEL_GROUPS):
        copy = pltpu.make_async_copy(back.at[group], blocks.at[group], in_sem.at[group])
        copy.start()
        copies.append(copy)
    leaving = []
    for group in range(VEL_GROUPS):
        copies[group].wait()

        @pl.loop(0, 2)
        def _(half):
            rows8 = pl.ds(pl.multiple_of(half * 8, 8), 8)

            def store(d, tile):
                done[group, d, rows8] = tile

            lane_swap(lambda p: blocks[group, p, rows8], store)

        for k, (owner, slot, row, count) in enumerate(PIECES):
            if owner == group:
                copy = pltpu.make_async_copy(
                    done.at[group, pl.ds(slot, count)], out.at[pl.ds(row, count)], out_sem.at[k]
                )
                copy.start()
                leaving.append(copy)
    for copy in leaving:
        copy.wait()


def shards(velocity, metric_terms, lift_scale, neighbour, neighbour_side, orientation):
    v = jnp.transpose(velocity, (0, 2, 1, 3)).reshape(3 * NN, LOCAL, ELEMS)
    metric = jnp.transpose(metric_terms, (1, 0, 2))
    lift = jnp.transpose(lift_scale, (0, 2, 1, 3)).reshape(2 * NP, 4, ELEMS)
    consts = [jnp.asarray(t) for t in tables()]
    anywhere = pl.BlockSpec(memory_space=pl.ANY)
    vmem = pltpu.VMEM
    dma = pltpu.SemaphoreType.DMA
    back = pl.pallas_call(
        main_kernel,
        out_shape=jax.ShapeDtypeStruct((VEL_GROUPS, MODES, LOCAL, 128), F32),
        in_specs=[anywhere] * 10,
        out_specs=anywhere,
        scratch_shapes=[
            vmem((3 * NN, LOCAL, 128), F32),
            vmem((GROUPS, 32, LOCAL, 128), F32),
            vmem((GROUPS, MODES, LOCAL, 128), F32),
            vmem((GROUPS, NZ, 128), F32),
            vmem((VEL_GROUPS, NZ, 128), F32),
            vmem((2 * NZ, 3 * NZ), BF16),
            vmem((NZ, 3 * NZ), BF16),
            vmem((768, 512), BF16),
            vmem((256, 512), BF16),
            vmem((NN, 8, 128), F32),
            vmem((2 * NP, 8, 128), F32),
            vmem((8, 128), jnp.int32),
            vmem((8, 128), jnp.int32),
            vmem((8, 128), jnp.int32),
            vmem((3, 224, 512), BF16),
            vmem((32, 512), BF16),
            vmem((512, 512), BF16),
            vmem((128, 512), BF16),
            vmem((512, 128), BF16),
            vmem((112, 128), F32),
            vmem((112, 128), F32),
            vmem((112, 128), F32),
            vmem((112, 128), F32),
            vmem((8, 256), F32),
            vmem((3, 3 * NZ, 256), BF16),
            vmem((3, 2 * NZ, 256), F32),
            vmem((NZ, 768), BF16),
            vmem((NZ, 512), F32),
            vmem((3, NZ, 256), F32),
            vmem((4, NZ, 256), F32),
            vmem((3 * NZ, 128), BF16),
            vmem((NZ, 256), BF16),
            vmem((3 * NZ, 256), BF16),
            vmem((3, NZ, 128), F32),
            dma((len(PIECES),)),
            dma((10,)),
            dma((GROUPS,)),
            dma((GROUPS,)),
            dma((VEL_GROUPS,)),
            dma((VEL_GROUPS,)),
            dma((2,)),
            dma((2,)),
        ],
        compiler_params=pltpu.CompilerParams(
            collective_id=0, has_side_effects=True, vmem_limit_bytes=62 << 20
        ),
        name="advect",
    )(v, metric, lift, neighbour, neighbour_side, orientation, *consts)
    out = pl.pallas_call(
        last_kernel,
        out_shape=jax.ShapeDtypeStruct((3 * NN, LOCAL, ELEMS), F32),
        in_specs=[anywhere],
        out_specs=anywhere,
        scratch_shapes=[
            vmem((VEL_GROUPS, MODES, LOCAL, 128), F32),
            vmem((VEL_GROUPS, 32, LOCAL, 128), F32),
            dma((VEL_GROUPS,)),
            dma((len(PIECES),)),
        ],
        compiler_params=pltpu.CompilerParams(vmem_limit_bytes=62 << 20),
        name="restore",
    )(back)
    return jnp.transpose(out.reshape(3, NN, LOCAL, ELEMS), (0, 2, 1, 3))


def solution(mesh):
    return jax.shard_map(
        shards,
        mesh=mesh,
        in_specs=(
            P(None, "mode", None, "plane"),
            P(None, None, "plane"),
            P(None, None, None, "plane"),
            P(None, "plane"),
            P(None, "plane"),
            P(None, "plane"),
        ),
        out_specs=P(None, "mode", None, "plane"),
        check_vma=False,
    )
```

```python
import jax
import jax.numpy as jnp
import ml_dtypes
import numpy as np
from jax import lax
from jax.experimental import pallas as pl
from jax.experimental.pallas import tpu as pltpu
from jax.sharding import PartitionSpec as P

MESH = pl.DeviceIdType.MESH
F32 = jnp.float32
BF16 = jnp.bfloat16

NP = 7
NN = 49
NZ = 512
MODES = 32
PLANES = 8
LOCAL = 16
ELEMS = 128
SPAN_WAVENUMBER = 0.25
VEL_GROUPS = 5
GROUPS = 8

GLL_POINTS = (
    -1.0,
    -0.830223896278567,
    -0.468848793470714,
    0.0,
    0.468848793470714,
    0.830223896278567,
    1.0,
)

PIECES = (
    (0, 0, 0, 32),
    (1, 0, 32, 17),
    (1, 17, 130, 15),
    (2, 0, 49, 32),
    (3, 0, 81, 17),
    (3, 17, 145, 2),
    (4, 0, 98, 32),
)


def derivative_matrix():
    points = np.array(GLL_POINTS)
    identity = np.eye(NP)
    offdiag = points[:, None] - points[None, :] + identity
    weights = 1.0 / np.prod(offdiag, axis=1)
    matrix = weights[None, :] / weights[:, None] / offdiag
    matrix = matrix * (1.0 - identity)
    return matrix - identity * matrix.sum(axis=1)[:, None]


def split_np(table):
    table = table.astype(np.float32)
    high = table.astype(ml_dtypes.bfloat16)
    low = (table - high.astype(np.float32)).astype(ml_dtypes.bfloat16)
    return high, low


def side_node(side, position):
    return (position, position * NP + NP - 1, (NP - 1) * NP + position, position * NP)[side]


def tables():
    index = np.arange(NZ)
    wave = np.where(index == 1, NZ // 2, index // 2)
    phase = (wave[:, None] * index[None, :] % NZ) * (2.0 * np.pi / NZ)
    sine_row = ((index % 2 == 1) & (index > 1))[:, None]
    inverse = np.where(sine_row, np.sin(phase), np.cos(phase))
    slope = np.where(index < 2, 0.0, wave)[:, None] * SPAN_WAVENUMBER
    slope = slope * np.where(sine_row, np.cos(phase), -np.sin(phase))
    high, low = split_np(np.concatenate([inverse.T, slope.T], axis=0))
    backward = np.concatenate([high, low, high], axis=1)
    high, low = split_np(inverse)
    forward = np.concatenate([high, low, high], axis=1)
    matrix = derivative_matrix()
    derive = np.zeros((256, 512))
    for j in range(NP):
        for i in range(NP):
            for b in range(NP):
                for e in range(4):
                    derive[4 * (j * NP + b) + e, 4 * (j * NP + i) + e] = matrix[i, b]
                    derive[4 * (b * NP + i) + e, 256 + 4 * (j * NP + i) + e] = matrix[j, b]
    high, low = split_np(derive)
    derive = np.concatenate([high, high, low], axis=0)
    place = np.zeros((128, 512))
    for side in range(4):
        for position in range(NP):
            for e in range(4):
                column = 4 * side_node(side, position) + e
                place[4 * (side * NP + position) + e, 256 * (side % 2) + column] = 1.0
    place = place.astype(ml_dtypes.bfloat16)
    return backward, forward, derive, np.concatenate([place, place], axis=0)


def halves(value):
    high = value.astype(BF16)
    return high, (value - high.astype(F32)).astype(BF16)


def lane_swap(load, store):
    lane = lax.broadcasted_iota(jnp.int32, (8, 128), 1)
    tiles = [None] * 32
    for p in range(32):
        tiles[-p % 32] = pltpu.roll(load(p), 4 * p, 1) if p else load(p)
    for bit in range(5):
        mask = (lane & (4 << bit)) != 0
        tiles = [jnp.where(mask, tiles[(j - (1 << bit)) % 32], tiles[j]) for j in range(32)]
    for d in range(32):
        store(d, pltpu.roll(tiles[d], 128 - 4 * d, 1) if d else tiles[d])


def matmul(a, b):
    return jnp.dot(a, b, preferred_element_type=F32)


def matmul_nt(a, b):
    return lax.dot_general(a, b, (((1,), (1,)), ((), ())), preferred_element_type=F32)


def exact(a, b):
    return jnp.dot(a, b, precision=lax.Precision.HIGHEST, preferred_element_type=F32)


def main_kernel(
    v_hbm,
    metric_hbm,
    lift_hbm,
    nb_hbm,
    ns_hbm,
    or_hbm,
    inv_hbm,
    fwd_hbm,
    der_hbm,
    place_hbm,
    out,
    back,
    done,
    vn,
    vs,
    sb,
    rx,
    sb2,
    inv,
    fwd,
    der,
    place,
    met,
    lif,
    nbv,
    nsv,
    orv,
    lmat,
    kmat,
    oh,
    sel,
    oht,
    up_out,
    dn_out,
    up_in,
    dn_in,
    rows,
    xr,
    pv,
    dlhs,
    dxe,
    base,
    uu,
    xa,
    la,
    xp,
    tail,
    load_sem,
    in_sem,
    send_sem,
    recv_sem,
    send2_sem,
    recv2_sem,
    halo_send,
    halo_recv,
    out_sem,
):
    me = lax.axis_index("mode")
    part = lax.axis_index("plane")
    above = lax.rem(part + 1, PLANES)
    below = lax.rem(part + PLANES - 1, PLANES)

    nbv[...] = jnp.full((8, 128), -1, jnp.int32)
    nsv[...] = jnp.zeros((8, 128), jnp.int32)
    orv[...] = jnp.zeros((8, 128), jnp.int32)
    met[...] = jnp.zeros_like(met)
    lif[...] = jnp.zeros_like(lif)
    loads = []
    for k, (group, slot, row, count) in enumerate(PIECES):
        copy = pltpu.make_async_copy(
            v_hbm.at[pl.ds(row, count)], vs.at[group, pl.ds(slot, count)], load_sem.at[k]
        )
        copy.start()
        loads.append((group, copy))
    others = []
    for k, (src, dst) in enumerate(
        (
            (v_hbm, vn),
            (nb_hbm, nbv.at[pl.ds(0, 4)]),
            (ns_hbm, nsv.at[pl.ds(0, 4)]),
            (or_hbm, orv.at[pl.ds(0, 4)]),
            (metric_hbm, met.at[:, pl.ds(0, 4)]),
            (lift_hbm, lif.at[:, pl.ds(0, 4)]),
            (inv_hbm, inv),
            (der_hbm, der),
            (place_hbm, place),
            (fwd_hbm, fwd),
        )
    ):
        copy = pltpu.make_async_copy(src, dst, in_sem.at[k])
        copy.start()
        others.append(copy)

    barrier = pltpu.get_barrier_semaphore()

    @pl.loop(1, MODES)
    def _(k):
        pl.semaphore_signal(
            barrier, inc=1, device_id={"mode": lax.rem(me + k, MODES)}, device_id_type=MESH
        )

    for other in (above, below):
        pl.semaphore_signal(barrier, inc=1, device_id={"plane": other}, device_id_type=MESH)

    vs[3, pl.ds(19, 13)] = jnp.zeros((13, LOCAL, 128), F32)
    for comp in range(3):
        vs[VEL_GROUPS + comp, pl.ds(28, 4)] = jnp.zeros((4, LOCAL, 128), F32)

    def scatter(group):
        @pl.loop(0, 2)
        def _(half):
            rows8 = pl.ds(pl.multiple_of(half * 8, 8), 8)

            def store(d, tile):
                sb[group, d, rows8] = tile

            lane_swap(lambda p: vs[group, p, rows8], store)

    def send(group):
        mine = rx.at[group, pl.ds(pl.multiple_of(me * LOCAL, LOCAL), LOCAL)]
        pltpu.make_async_copy(sb.at[group, me], mine, recv_sem.at[group]).start()

        @pl.loop(1, MODES)
        def _(k):
            to = lax.rem(me + k, MODES)
            pltpu.make_async_remote_copy(
                src_ref=sb.at[group, to],
                dst_ref=mine,
                send_sem=send_sem.at[group],
                recv_sem=recv_sem.at[group],
                device_id={"mode": to},
                device_id_type=MESH,
            ).start()

    for group in range(VEL_GROUPS):
        for owner, copy in loads:
            if owner == group:
                copy.wait()
        scatter(group)
        if group == 0:
            pl.semaphore_wait(barrier, MODES + 1)
        send(group)

    for copy in others[:4]:
        copy.wait()
    nb = nbv[...]
    exists = nb >= 0
    owner = lax.shift_right_arithmetic(nb, 7)
    target = nsv[...] * ELEMS + (nb & (ELEMS - 1))
    own_key = jnp.where(exists & (owner == part), target, -1)
    is_up = exists & (owner == part + 1)
    is_dn = exists & (owner == part - 1)
    strict = (
        lax.broadcasted_iota(jnp.int32, (128, 128), 0)
        < lax.broadcasted_iota(jnp.int32, (128, 128), 1)
    ).astype(F32)
    ranks = []
    for border in (is_up, is_dn):
        flag = jnp.where(border, 1.0, 0.0)
        before = exact(flag, strict)
        totals = jnp.sum(flag, axis=1, keepdims=True)
        offset = jnp.zeros((1, 1), F32)
        found = []
        for side in range(4):
            found.append(before[side : side + 1] + offset)
            offset = offset + totals[side : side + 1]
        ranks.append(found)
    row128 = lax.broadcasted_iota(jnp.int32, (128, 128), 0).astype(F32)
    row512 = lax.broadcasted_iota(jnp.int32, (512, 128), 0)
    for side in range(4):
        lanes = pl.ds(side * 128, 128)
        one = slice(side, side + 1)
        slot = jnp.where(
            is_up[one], ranks[0][side], jnp.where(is_dn[one], 32.0 + ranks[1][side], -1.0)
        )
        sel[:, lanes] = jnp.where(row128 == slot, 1.0, 0.0).astype(BF16)
        oh[:, lanes] = jnp.where(row512 == own_key[one], 1.0, 0.0).astype(BF16)
        high, low = halves(jnp.broadcast_to((target[one] + 1).astype(F32), (16, 128)))
        kmat[pl.ds(0, 16), lanes] = high
        kmat[pl.ds(16, 16), lanes] = low
    turned = orv[...] == 1

    @pl.loop(0, 3)
    def _(comp):
        for position in range(NP):
            for side in range(4):
                straight = vn[comp * NN + side_node(side, position)]
                reverse = vn[comp * NN + side_node(side, NP - 1 - position)]
                value = jnp.where(turned[side : side + 1], reverse, straight)
                high, low = halves(value)
                lanes = pl.ds(side * 128, 128)
                lmat[comp, pl.ds(position * 16, 16), lanes] = high
                lmat[comp, pl.ds(112 + position * 16, 16), lanes] = low

    picked = []
    for comp in range(3):
        both = matmul_nt(lmat[comp], sel[...])
        picked.append(both[:112] + both[112:])
    both = matmul_nt(kmat[...], sel[...])
    keys = jnp.concatenate([both[:16] + both[16:], jnp.zeros((96, 128), F32)], axis=0)
    picked.append(keys)
    lane = lax.broadcasted_iota(jnp.int32, (112, 128), 1)
    for ref, shift in ((up_out, 0), (dn_out, 96)):
        packed = None
        for k in (3, 2, 1, 0):
            by = (32 * k + shift) % 128
            moved = pltpu.roll(picked[k], by, 1) if by else picked[k]
            packed = moved if packed is None else jnp.where(lane < 32 * k + 32, moved, packed)
        ref[...] = packed
    halo = []
    for k, (src, dst, to) in enumerate(((up_out, up_in, above), (dn_out, dn_in, below))):
        copy = pltpu.make_async_remote_copy(
            src_ref=src,
            dst_ref=dst,
            send_sem=halo_send.at[k],
            recv_sem=halo_recv.at[k],
            device_id={"plane": to},
            device_id_type=MESH,
        )
        copy.start()
        halo.append(copy)

    for copy in others[4:6]:
        copy.wait()
    fold = (
        lax.broadcasted_iota(jnp.int32, (128, 256), 0)
        == 4 * me + (lax.broadcasted_iota(jnp.int32, (128, 256), 1) & 3)
    ).astype(F32)
    spread = exact(met[...].reshape(NN * 8, 128), fold).reshape(NN, 8, 256)
    node3 = lax.shift_right_arithmetic(lax.broadcasted_iota(jnp.int32, (NN, 8, 256), 2), 2)
    here = node3 == lax.broadcasted_iota(jnp.int32, (NN, 8, 256), 0)
    metric_rows = jnp.sum(jnp.where(here, spread, 0.0), axis=0)
    rows[pl.ds(0, 4)] = metric_rows[:4]
    live = exact(jnp.where(exists, 0.5, 0.0), fold)
    spread = exact(lif[...].reshape(2 * NP * 8, 128), fold).reshape(2 * NP, 8, 256)
    node2 = lax.shift_right_arithmetic(lax.broadcasted_iota(jnp.int32, (8, 256), 1), 2)
    side2 = lax.broadcasted_iota(jnp.int32, (8, 256), 0)
    for axis in range(2):
        total = jnp.zeros((8, 256), F32)
        for position in range(NP):
            wanted = jnp.full((8, 256), -1, jnp.int32)
            for side in range(4):
                wanted = jnp.where(side2 == side, side_node(side, position), wanted)
            total = total + jnp.where(node2 == wanted, spread[axis * NP + position], 0.0)
        total = total * live
        rows[pl.ds(4 + axis, 1)] = total[0:1] + total[2:3]
        rows[pl.ds(6 + axis, 1)] = total[1:2] + total[3:4]

    for copy in halo:
        copy.wait_recv()
    lane1 = lax.broadcasted_iota(jnp.int32, (8, 128), 1)
    key_up = pltpu.roll(up_in[pl.ds(0, 8)], 32, 1)
    key_dn = pltpu.roll(dn_in[pl.ds(0, 8)], 64, 1)
    key = jnp.where(lane1 < 32, key_up, jnp.where(lane1 < 64, key_dn, 0.0))[0:1]
    oht[...] = jnp.where((row512 + 1).astype(F32) == key, 1.0, 0.0).astype(BF16)
    for comp in range(3):
        both = matmul(lmat[comp], oh[...])
        across = both[:112] + both[112:]
        from_up = pltpu.roll(up_in[...], (128 - 32 * comp) % 128, 1) if comp else up_in[...]
        from_dn = pltpu.roll(dn_in[...], (160 - 32 * comp) % 128, 1) if comp != 1 else dn_in[...]
        high, low = halves(jnp.where(lane < 32, from_up, jnp.where(lane < 64, from_dn, 0.0)))
        both = matmul_nt(jnp.concatenate([high, low], axis=0), oht[...])
        across = across + (both[:112] + both[112:])
        for side in range(4):
            for position in range(NP):
                vs[VEL_GROUPS + comp, side * NP + position] = across[
                    position * 16 : position * 16 + 16, side * 128 : side * 128 + 128
                ]
        scatter(VEL_GROUPS + comp)
        send(VEL_GROUPS + comp)

    def received(group):
        pltpu.make_async_copy(rx.at[group], rx.at[group], recv_sem.at[group]).wait()

    for copy in others[6:]:
        copy.wait()
    lane64 = lax.broadcasted_iota(jnp.int32, (64, 128), 1)

    def on_planes(comp, pieces):
        @pl.loop(0, 8)
        def _(block):
            at = pl.multiple_of(block * 64, 64)
            for k in range(2):
                high, low = halves(pieces[k](pl.ds(at, 64)))
                lanes = pl.ds(k * 128, 128)
                xr[pl.ds(at, 64), lanes] = high
                xr[pl.ds(at + 512, 64), lanes] = high
                xr[pl.ds(at + 1024, 64), lanes] = low

        pv[comp] = matmul(inv[...], xr[...])

        @pl.loop(0, 8)
        def _(block):
            rows64 = pl.ds(pl.multiple_of(block * 64, 64), 64)
            high, low = halves(pv[comp, rows64])
            dlhs[rows64, pl.ds(0, 256)] = high
            dlhs[rows64, pl.ds(256, 256)] = low
            dlhs[rows64, pl.ds(512, 256)] = high

        dxe[comp] = matmul(dlhs[...], der[...])

    def joined(rows64):
        return jnp.where(
            lane64 < 60, pltpu.roll(rx[1, rows64], 60, 1), pltpu.roll(rx[3, rows64], 120, 1)
        )

    received(0)
    received(1)
    on_planes(0, (lambda r: rx[0, r], lambda r: rx[1, r]))
    received(2)
    received(3)
    on_planes(1, (lambda r: rx[2, r], lambda r: rx[3, r]))
    received(4)
    on_planes(2, (lambda r: rx[4, r], joined))

    @pl.loop(0, 16)
    def _(block):
        at = pl.multiple_of(block * 32, 32)
        rows32 = pl.ds(at, 32)
        u, v, w = pv[0, rows32], pv[1, rows32], pv[2, rows32]
        first = u * rows[pl.ds(0, 1)] + v * rows[pl.ds(1, 1)]
        second = u * rows[pl.ds(2, 1)] + v * rows[pl.ds(3, 1)]
        layer_a = u * rows[pl.ds(4, 1)] + v * rows[pl.ds(5, 1)]
        layer_b = u * rows[pl.ds(6, 1)] + v * rows[pl.ds(7, 1)]
        uu[0, rows32] = layer_a
        uu[1, rows32] = layer_b
        layer_b = layer_a + layer_b
        for comp in range(3):
            total = first * dxe[comp, rows32, pl.ds(0, 256)]
            total = total + second * dxe[comp, rows32, pl.ds(256, 256)]
            total = total + w * pv[comp, pl.ds(at + 512, 32)]
            base[comp, rows32] = total - layer_b * pv[comp, rows32]

    def send_back(group):
        pltpu.make_async_copy(
            sb2.at[group, pl.ds(pl.multiple_of(me * LOCAL, LOCAL), LOCAL)],
            back.at[group, me],
            recv2_sem.at[group],
        ).start()

        @pl.loop(1, MODES)
        def _(k):
            to = lax.rem(me + k, MODES)
            pltpu.make_async_remote_copy(
                src_ref=sb2.at[group, pl.ds(pl.multiple_of(to * LOCAL, LOCAL), LOCAL)],
                dst_ref=back.at[group, me],
                send_sem=send2_sem.at[group],
                recv_sem=recv2_sem.at[group],
                device_id={"mode": to},
                device_id_type=MESH,
            ).start()

    @pl.loop(0, 3)
    def _(comp):
        received(VEL_GROUPS + comp)

        @pl.loop(0, 8)
        def _(block):
            at = pl.multiple_of(block * 64, 64)
            high, low = halves(rx[VEL_GROUPS + comp, pl.ds(at, 64)])
            xa[pl.ds(at, 64)] = high
            xa[pl.ds(at + 512, 64)] = high
            xa[pl.ds(at + 1024, 64)] = low

        high, low = halves(matmul(inv[pl.ds(0, 512)], xa[...]))
        la[:, pl.ds(0, 128)] = high
        la[:, pl.ds(128, 128)] = low
        dxe[0] = matmul(la[...], place[...])

        @pl.loop(0, 8)
        def _(block):
            at = pl.multiple_of(block * 64, 64)
            rows64 = pl.ds(at, 64)
            total = base[comp, rows64] + uu[0, rows64] * dxe[0, rows64, pl.ds(0, 256)]
            total = total + uu[1, rows64] * dxe[0, rows64, pl.ds(256, 256)]
            high, low = halves(total)
            xp[rows64] = high
            xp[pl.ds(at + 512, 64)] = high
            xp[pl.ds(at + 1024, 64)] = low

        result = matmul(fwd[...], xp[...])
        sb2[2 * comp] = result[:, :128]
        tail[comp] = result[:, 128:]
        send_back(2 * comp)

    @pl.loop(0, 8)
    def _(block):
        rows64 = pl.ds(pl.multiple_of(block * 64, 64), 64)
        last = tail[2, rows64]
        sb2[1, rows64] = jnp.where(lane64 < 68, tail[0, rows64], pltpu.roll(last, 68, 1))
        sb2[3, rows64] = jnp.where(lane64 < 68, tail[1, rows64], pltpu.roll(last, 8, 1))

    send_back(1)
    send_back(3)

    leaving = []
    for group in (0, 2, 4, 1, 3):
        pltpu.make_async_copy(back.at[group], back.at[group], recv2_sem.at[group]).wait()

        @pl.loop(0, 2)
        def _(half):
            rows8 = pl.ds(pl.multiple_of(half * 8, 8), 8)

            def store(d, tile):
                done[group, d, rows8] = tile

            lane_swap(lambda p: back[group, p, rows8], store)

        for k, (owner, slot, row, count) in enumerate(PIECES):
            if owner == group:
                copy = pltpu.make_async_copy(
                    done.at[group, pl.ds(slot, count)], out.at[pl.ds(row, count)], out_sem.at[k]
                )
                copy.start()
                leaving.append(copy)

    for copy in halo:
        copy.wait_send()
    for group in range(GROUPS):
        sent = sb.at[group, pl.ds(0, MODES - 1)]
        pltpu.make_async_copy(sent, sent, send_sem.at[group]).wait()
    for group in range(VEL_GROUPS):
        sent = sb2.at[group, pl.ds(0, (MODES - 1) * LOCAL)]
        pltpu.make_async_copy(sent, sent, send2_sem.at[group]).wait()
    for copy in leaving:
        copy.wait()


def shards(velocity, metric_terms, lift_scale, neighbour, neighbour_side, orientation):
    v = jnp.transpose(velocity, (0, 2, 1, 3)).reshape(3 * NN, LOCAL, ELEMS)
    metric = jnp.transpose(metric_terms, (1, 0, 2))
    lift = jnp.transpose(lift_scale, (0, 2, 1, 3)).reshape(2 * NP, 4, ELEMS)
    operands = [v, metric, lift, neighbour, neighbour_side, orientation]
    operands += [jnp.asarray(t) for t in tables()]
    anywhere = pl.BlockSpec(memory_space=pl.ANY)
    vmem = pltpu.VMEM
    dma = pltpu.SemaphoreType.DMA
    out = pl.pallas_call(
        main_kernel,
        out_shape=pltpu.VMEM((3 * NN, LOCAL, ELEMS), F32),
        in_specs=[anywhere] * 10,
        out_specs=anywhere,
        scratch_shapes=[
            vmem((VEL_GROUPS, MODES, LOCAL, 128), F32),
            vmem((VEL_GROUPS, 32, LOCAL, 128), F32),
            vmem((3 * NN, LOCAL, 128), F32),
            vmem((GROUPS, 32, LOCAL, 128), F32),
            vmem((GROUPS, MODES, LOCAL, 128), F32),
            vmem((GROUPS, NZ, 128), F32),
            vmem((VEL_GROUPS, NZ, 128), F32),
            vmem((2 * NZ, 3 * NZ), BF16),
            vmem((NZ, 3 * NZ), BF16),
            vmem((768, 512), BF16),
            vmem((256, 512), BF16),
            vmem((NN, 8, 128), F32),
            vmem((2 * NP, 8, 128), F32),
            vmem((8, 128), jnp.int32),
            vmem((8, 128), jnp.int32),
            vmem((8, 128), jnp.int32),
            vmem((3, 224, 512), BF16),
            vmem((32, 512), BF16),
            vmem((512, 512), BF16),
            vmem((128, 512), BF16),
            vmem((512, 128), BF16),
            vmem((112, 128), F32),
            vmem((112, 128), F32),
            vmem((112, 128), F32),
            vmem((112, 128), F32),
            vmem((8, 256), F32),
            vmem((3 * NZ, 256), BF16),
            vmem((3, 2 * NZ, 256), F32),
            vmem((NZ, 768), BF16),
            vmem((3, NZ, 512), F32),
            vmem((3, NZ, 256), F32),
            vmem((2, NZ, 256), F32),
            vmem((3 * NZ, 128), BF16),
            vmem((NZ, 256), BF16),
            vmem((3 * NZ, 256), BF16),
            vmem((3, NZ, 128), F32),
            dma((len(PIECES),)),
            dma((10,)),
            dma((GROUPS,)),
            dma((GROUPS,)),
            dma((VEL_GROUPS,)),
            dma((VEL_GROUPS,)),
            dma((2,)),
            dma((2,)),
            dma((len(PIECES),)),
        ],
        compiler_params=pltpu.CompilerParams(
            collective_id=0, has_side_effects=True, vmem_limit_bytes=48 << 20
        ),
        name="advect",
    )(*[pltpu.with_memory_space_constraint(x, pltpu.HBM) for x in operands])
    index = lax.axis_index("mode") * LOCAL + jnp.arange(LOCAL, dtype=jnp.int32)
    weighting = jnp.where(index < 2, 1.0 / NZ, 2.0 / NZ).astype(F32)
    out = out.reshape(3, NN, LOCAL, ELEMS) * weighting[:, None]
    return jnp.transpose(out, (0, 2, 1, 3))


def solution(mesh):
    return jax.shard_map(
        shards,
        mesh=mesh,
        in_specs=(
            P(None, "mode", None, "plane"),
            P(None, None, "plane"),
            P(None, None, None, "plane"),
            P(None, "plane"),
            P(None, "plane"),
            P(None, "plane"),
        ),
        out_specs=P(None, "mode", None, "plane"),
        check_vma=False,
    )
```

```python
import jax
import jax.numpy as jnp
import ml_dtypes
import numpy as np
from jax import lax
from jax.experimental import pallas as pl
from jax.experimental.pallas import tpu as pltpu
from jax.sharding import PartitionSpec as P

MESH = pl.DeviceIdType.MESH
F32 = jnp.float32
BF16 = jnp.bfloat16

NP = 7
NN = 49
NZ = 512
MODES = 32
PLANES = 8
LOCAL = 16
ELEMS = 128
SPAN_WAVENUMBER = 0.25
GROUPS = 6

GLL_POINTS = (
    -1.0,
    -0.830223896278567,
    -0.468848793470714,
    0.0,
    0.468848793470714,
    0.830223896278567,
    1.0,
)

PIECES = (
    (0, 0, 0, 32),
    (3, 0, 32, 17),
    (3, 17, 81, 15),
    (1, 0, 49, 32),
    (4, 0, 130, 17),
    (4, 17, 96, 2),
    (2, 0, 98, 32),
)
TRACES = (
    (0, 0, 13, 4, 19),
    (0, 13, 15, 6, 0),
    (1, 0, 28, 5, 0),
    (2, 0, 4, 5, 28),
    (2, 4, 16, 7, 0),
    (2, 20, 8, 8, 0),
)
RETURNS = (
    tuple(range(0, 32)),
    tuple(range(49, 81)),
    tuple(range(98, 130)),
    tuple(range(32, 49)) + tuple(range(81, 96)),
)
HALF = tuple(range(130, 146))
QUARTER = (146, 96, 97)


def derivative_matrix():
    points = np.array(GLL_POINTS)
    identity = np.eye(NP)
    offdiag = points[:, None] - points[None, :] + identity
    weights = 1.0 / np.prod(offdiag, axis=1)
    matrix = weights[None, :] / weights[:, None] / offdiag
    matrix = matrix * (1.0 - identity)
    return matrix - identity * matrix.sum(axis=1)[:, None]


def split_np(table):
    table = table.astype(np.float32)
    high = table.astype(ml_dtypes.bfloat16)
    low = (table - high.astype(np.float32)).astype(ml_dtypes.bfloat16)
    return high, low


def side_node(side, position):
    return (position, position * NP + NP - 1, (NP - 1) * NP + position, position * NP)[side]


def tables():
    index = np.arange(NZ)
    wave = np.where(index == 1, NZ // 2, index // 2)
    phase = (wave[:, None] * index[None, :] % NZ) * (2.0 * np.pi / NZ)
    sine_row = ((index % 2 == 1) & (index > 1))[:, None]
    inverse = np.where(sine_row, np.sin(phase), np.cos(phase))
    slope = np.where(index < 2, 0.0, wave)[:, None] * SPAN_WAVENUMBER
    slope = slope * np.where(sine_row, np.cos(phase), -np.sin(phase))
    high, low = split_np(np.concatenate([inverse.T, slope.T], axis=0))
    backward = np.concatenate([high, low, high], axis=1)
    high, low = split_np(inverse)
    forward = np.concatenate([high, low, high], axis=1)
    matrix = derivative_matrix()
    derive = np.zeros((256, 512))
    for j in range(NP):
        for i in range(NP):
            for b in range(NP):
                for e in range(4):
                    derive[4 * (j * NP + b) + e, 4 * (j * NP + i) + e] = matrix[i, b]
                    derive[4 * (b * NP + i) + e, 256 + 4 * (j * NP + i) + e] = matrix[j, b]
    high, low = split_np(derive)
    derive = np.concatenate([high, high, low], axis=0)
    place = np.zeros((3, 256, 512))
    starts = {(0, 0): 76, (0, 13): 128, (1, 0): 0, (2, 0): 112, (2, 4): 128, (2, 20): 192}
    for comp, first, count, _, _ in TRACES:
        for k in range(count):
            side, position = divmod(first + k, NP)
            for e in range(4):
                column = 256 * (side % 2) + 4 * side_node(side, position) + e
                place[comp, starts[comp, first] + 4 * k + e, column] = 1.0
    place = place.astype(ml_dtypes.bfloat16)
    place[1, 128:] = place[1, :128]
    return backward, forward, derive, np.concatenate([place, place], axis=1)


def halves(value):
    high = value.astype(BF16)
    return high, (value - high.astype(F32)).astype(BF16)


def lane_swap(load, store):
    lane = lax.broadcasted_iota(jnp.int32, (8, 128), 1)
    tiles = [None] * 32
    for p in range(32):
        tiles[-p % 32] = pltpu.roll(load(p), 4 * p, 1) if p else load(p)
    for bit in range(5):
        mask = (lane & (4 << bit)) != 0
        tiles = [jnp.where(mask, tiles[(j - (1 << bit)) % 32], tiles[j]) for j in range(32)]
    for d in range(32):
        store(d, pltpu.roll(tiles[d], 128 - 4 * d, 1) if d else tiles[d])


def matmul(a, b):
    return jnp.dot(a, b, preferred_element_type=F32)


def matmul_nt(a, b):
    return lax.dot_general(a, b, (((1,), (1,)), ((), ())), preferred_element_type=F32)


def exact(a, b):
    return jnp.dot(a, b, precision=lax.Precision.HIGHEST, preferred_element_type=F32)


def main_kernel(
    v_hbm,
    metric_hbm,
    lift_hbm,
    nb_hbm,
    ns_hbm,
    or_hbm,
    inv_hbm,
    fwd_hbm,
    der_hbm,
    place_hbm,
    out,
    back,
    back_h,
    back_q,
    done,
    vn,
    vs,
    vp,
    sb,
    sp,
    rx,
    rp,
    sb2,
    sh2,
    sq2,
    inv,
    fwd,
    der,
    place,
    met,
    lif,
    nbv,
    nsv,
    orv,
    lmat,
    kmat,
    oh,
    sel,
    oht,
    up_out,
    dn_out,
    up_in,
    dn_in,
    rows,
    xr,
    pv,
    dlhs,
    dxe,
    base,
    uu,
    xa,
    pa,
    la,
    xp,
    tail,
    load_sem,
    in_sem,
    send_sem,
    recv_sem,
    send2_sem,
    recv2_sem,
    halo_send,
    halo_recv,
    out_sem,
    ready_sem,
):
    me = lax.axis_index("mode")
    part = lax.axis_index("plane")
    has_above = part < PLANES - 1
    has_below = part > 0
    above = lax.rem(part + 1, PLANES)
    below = lax.rem(part + PLANES - 1, PLANES)

    barrier = pltpu.get_barrier_semaphore()

    @pl.loop(1, MODES)
    def _(k):
        pl.semaphore_signal(
            barrier, inc=1, device_id={"mode": lax.rem(me + k, MODES)}, device_id_type=MESH
        )

    @pl.when(has_above)
    def _():
        pl.semaphore_signal(barrier, inc=1, device_id={"plane": above}, device_id_type=MESH)

    def entered():
        @pl.when(has_below)
        def _():
            pl.semaphore_wait(barrier, MODES)
            pl.semaphore_signal(ready_sem, inc=1, device_id={"plane": below}, device_id_type=MESH)

        @pl.when(part == 0)
        def _():
            pl.semaphore_wait(barrier, MODES - 1)

    nbv[...] = jnp.full((8, 128), -1, jnp.int32)
    nsv[...] = jnp.zeros((8, 128), jnp.int32)
    orv[...] = jnp.zeros((8, 128), jnp.int32)
    met[...] = jnp.zeros_like(met)
    lif[...] = jnp.zeros_like(lif)
    loads = []
    for k, (group, slot, row, count) in enumerate(PIECES):
        copy = pltpu.make_async_copy(
            v_hbm.at[pl.ds(row, count)], vs.at[group, pl.ds(slot, count)], load_sem.at[k]
        )
        copy.start()
        loads.append((group, copy))
    others = []
    for k, (src, dst) in enumerate(
        (
            (v_hbm, vn),
            (nb_hbm, nbv.at[pl.ds(0, 4)]),
            (ns_hbm, nsv.at[pl.ds(0, 4)]),
            (or_hbm, orv.at[pl.ds(0, 4)]),
            (metric_hbm, met.at[:, pl.ds(0, 4)]),
            (lift_hbm, lif.at[:, pl.ds(0, 4)]),
            (inv_hbm, inv),
            (der_hbm, der),
            (place_hbm, place),
            (fwd_hbm, fwd),
        )
    ):
        copy = pltpu.make_async_copy(src, dst, in_sem.at[k])
        copy.start()
        others.append(copy)

    vp[...] = jnp.zeros_like(vp)

    @pl.when(part == 0)
    def _():
        up_in[...] = jnp.zeros_like(up_in)

    @pl.when(part == PLANES - 1)
    def _():
        dn_in[...] = jnp.zeros_like(dn_in)

    def scatter(group):
        @pl.loop(0, 2)
        def _(half):
            rows8 = pl.ds(pl.multiple_of(half * 8, 8), 8)

            def store(d, tile):
                sb[group, d, rows8] = tile

            lane_swap(lambda p: vs[group, p, rows8], store)

    def send(group):
        mine = rx.at[group, pl.ds(pl.multiple_of(me * LOCAL, LOCAL), LOCAL)]
        pltpu.make_async_copy(sb.at[group, me], mine, recv_sem.at[group]).start()

        @pl.loop(1, MODES)
        def _(k):
            to = lax.rem(me + k, MODES)
            pltpu.make_async_remote_copy(
                src_ref=sb.at[group, to],
                dst_ref=mine,
                send_sem=send_sem.at[group],
                recv_sem=recv_sem.at[group],
                device_id={"mode": to},
                device_id_type=MESH,
            ).start()

    def depart(group):
        for owner, copy in loads:
            if owner == group:
                copy.wait()
        scatter(group)
        if group == 0:
            entered()
        send(group)

    def part_rows(group):
        return pl.ds(0, 4 if group == 8 else 8)

    def depart_part(group):
        k = group - GROUPS

        def store(d, tile):
            sp[k, d] = tile

        lane_swap(lambda p: vp[k, p], store)
        some = part_rows(group)
        pltpu.make_async_copy(sp.at[k, me, some], rp.at[k, me, some], recv_sem.at[group]).start()

        @pl.loop(1, MODES)
        def _(j):
            to = lax.rem(me + j, MODES)
            pltpu.make_async_remote_copy(
                src_ref=sp.at[k, to, some],
                dst_ref=rp.at[k, me, some],
                send_sem=send_sem.at[group],
                recv_sem=recv_sem.at[group],
                device_id={"mode": to},
                device_id_type=MESH,
            ).start()

    for group in (0, 3, 1):
        depart(group)

    for copy in others[:4]:
        copy.wait()
    nb = nbv[...]
    exists = nb >= 0
    owner = lax.shift_right_arithmetic(nb, 7)
    target = nsv[...] * ELEMS + (nb & (ELEMS - 1))
    own_key = jnp.where(exists & (owner == part), target, -1)
    is_up = exists & (owner == part + 1)
    is_dn = exists & (owner == part - 1)
    strict = (
        lax.broadcasted_iota(jnp.int32, (128, 128), 0)
        < lax.broadcasted_iota(jnp.int32, (128, 128), 1)
    ).astype(F32)
    ranks = []
    for border in (is_up, is_dn):
        flag = jnp.where(border, 1.0, 0.0)
        before = exact(flag, strict)
        totals = jnp.sum(flag, axis=1, keepdims=True)
        offset = jnp.zeros((1, 1), F32)
        found = []
        for side in range(4):
            found.append(before[side : side + 1] + offset)
            offset = offset + totals[side : side + 1]
        ranks.append(found)
    row128 = lax.broadcasted_iota(jnp.int32, (128, 128), 0).astype(F32)
    row512 = lax.broadcasted_iota(jnp.int32, (512, 128), 0)
    for side in range(4):
        lanes = pl.ds(side * 128, 128)
        one = slice(side, side + 1)
        slot = jnp.where(
            is_up[one], ranks[0][side], jnp.where(is_dn[one], 32.0 + ranks[1][side], -1.0)
        )
        sel[:, lanes] = jnp.where(row128 == slot, 1.0, 0.0).astype(BF16)
        oh[:, lanes] = jnp.where(row512 == own_key[one], 1.0, 0.0).astype(BF16)
        high, low = halves(jnp.broadcast_to((target[one] + 1).astype(F32), (16, 128)))
        kmat[pl.ds(0, 16), lanes] = high
        kmat[pl.ds(16, 16), lanes] = low
    turned = orv[...] == 1

    @pl.loop(0, 3)
    def _(comp):
        for position in range(NP):
            for side in range(4):
                straight = vn[comp * NN + side_node(side, position)]
                reverse = vn[comp * NN + side_node(side, NP - 1 - position)]
                value = jnp.where(turned[side : side + 1], reverse, straight)
                high, low = halves(value)
                lanes = pl.ds(side * 128, 128)
                lmat[comp, pl.ds(position * 16, 16), lanes] = high
                lmat[comp, pl.ds(112 + position * 16, 16), lanes] = low

    picked = []
    for comp in range(3):
        both = matmul_nt(lmat[comp], sel[...])
        picked.append(both[:112] + both[112:])
    both = matmul_nt(kmat[...], sel[...])
    keys = jnp.concatenate([both[:16] + both[16:], jnp.zeros((96, 128), F32)], axis=0)
    picked.append(keys)
    lane = lax.broadcasted_iota(jnp.int32, (112, 128), 1)
    for ref, shift in ((up_out, 0), (dn_out, 96)):
        packed = None
        for k in (3, 2, 1, 0):
            by = (32 * k + shift) % 128
            moved = pltpu.roll(picked[k], by, 1) if by else picked[k]
            packed = moved if packed is None else jnp.where(lane < 32 * k + 32, moved, packed)
        ref[...] = packed
    halo = [
        pltpu.make_async_remote_copy(
            src_ref=src,
            dst_ref=dst,
            send_sem=halo_send.at[k],
            recv_sem=halo_recv.at[k],
            device_id={"plane": to},
            device_id_type=MESH,
        )
        for k, (src, dst, to) in enumerate(((up_out, up_in, above), (dn_out, dn_in, below)))
    ]

    @pl.when(has_below)
    def _():
        halo[1].start()

    @pl.when(has_above)
    def _():
        pl.semaphore_wait(ready_sem, 1)
        halo[0].start()

    for copy in others[4:6]:
        copy.wait()
    fold = (
        lax.broadcasted_iota(jnp.int32, (128, 256), 0)
        == 4 * me + (lax.broadcasted_iota(jnp.int32, (128, 256), 1) & 3)
    ).astype(F32)
    spread = exact(met[...].reshape(NN * 8, 128), fold).reshape(NN, 8, 256)
    node3 = lax.shift_right_arithmetic(lax.broadcasted_iota(jnp.int32, (NN, 8, 256), 2), 2)
    here = node3 == lax.broadcasted_iota(jnp.int32, (NN, 8, 256), 0)
    metric_rows = jnp.sum(jnp.where(here, spread, 0.0), axis=0)
    rows[pl.ds(0, 4)] = metric_rows[:4]
    live = exact(jnp.where(exists, 0.5, 0.0), fold)
    spread = exact(lif[...].reshape(2 * NP * 8, 128), fold).reshape(2 * NP, 8, 256)
    node2 = lax.shift_right_arithmetic(lax.broadcasted_iota(jnp.int32, (8, 256), 1), 2)
    side2 = lax.broadcasted_iota(jnp.int32, (8, 256), 0)
    for axis in range(2):
        total = jnp.zeros((8, 256), F32)
        for position in range(NP):
            wanted = jnp.full((8, 256), -1, jnp.int32)
            for side in range(4):
                wanted = jnp.where(side2 == side, side_node(side, position), wanted)
            total = total + jnp.where(node2 == wanted, spread[axis * NP + position], 0.0)
        total = total * live
        rows[pl.ds(4 + axis, 1)] = total[0:1] + total[2:3]
        rows[pl.ds(6 + axis, 1)] = total[1:2] + total[3:4]

    @pl.when(has_below)
    def _():
        halo[0].wait_recv()

    @pl.when(has_above)
    def _():
        halo[1].wait_recv()

    lane1 = lax.broadcasted_iota(jnp.int32, (8, 128), 1)
    key_up = pltpu.roll(up_in[pl.ds(0, 8)], 32, 1)
    key_dn = pltpu.roll(dn_in[pl.ds(0, 8)], 64, 1)
    key = jnp.where(lane1 < 32, key_up, jnp.where(lane1 < 64, key_dn, 0.0))[0:1]
    oht[...] = jnp.where((row512 + 1).astype(F32) == key, 1.0, 0.0).astype(BF16)
    for comp in range(3):
        both = matmul(lmat[comp], oh[...])
        across = both[:112] + both[112:]
        from_up = pltpu.roll(up_in[...], (128 - 32 * comp) % 128, 1) if comp else up_in[...]
        from_dn = pltpu.roll(dn_in[...], (160 - 32 * comp) % 128, 1) if comp != 1 else dn_in[...]
        high, low = halves(jnp.where(lane < 32, from_up, jnp.where(lane < 64, from_dn, 0.0)))
        both = matmul_nt(jnp.concatenate([high, low], axis=0), oht[...])
        across = across + (both[:112] + both[112:])
        for owner, first, count, group, slot in TRACES:
            if owner != comp:
                continue
            for k in range(count):
                side, position = divmod(first + k, NP)
                lanes = slice(side * 128, side * 128 + 128)
                where = slice(position * 16, position * 16 + 16)
                if group < GROUPS:
                    vs[group, slot + k] = across[where, lanes]
                    continue
                parts = 4 if group == 8 else 2
                for part_at in range(parts):
                    size = 16 // parts
                    at = position * 16 + part_at * size
                    vp[group - GROUPS, part_at * (32 // parts) + k, pl.ds(0, size)] = across[
                        at : at + size, lanes
                    ]
        if comp == 0:
            depart(4)
            depart(2)
            depart_part(6)
        elif comp == 1:
            continue
        else:
            depart(5)
            depart_part(7)
            depart_part(8)

    def received(group):
        ref = rx.at[group] if group < GROUPS else rp.at[group - GROUPS, :, part_rows(group)]
        pltpu.make_async_copy(ref, ref, recv_sem.at[group]).wait()

    for copy in others[6:]:
        copy.wait()
    lane64 = lax.broadcasted_iota(jnp.int32, (64, 128), 1)

    def gather(pieces):
        @pl.loop(0, 8)
        def _(block):
            at = pl.multiple_of(block * 64, 64)
            for k in range(2):
                high, low = halves(pieces[k](pl.ds(at, 64)))
                lanes = pl.ds(k * 128, 128)
                xr[pl.ds(at, 64), lanes] = high
                xr[pl.ds(at + 512, 64), lanes] = high
                xr[pl.ds(at + 1024, 64), lanes] = low

    def derive(comp):
        @pl.loop(0, 8)
        def _(block):
            rows64 = pl.ds(pl.multiple_of(block * 64, 64), 64)
            high, low = halves(pv[comp, rows64])
            dlhs[rows64, pl.ds(0, 256)] = high
            dlhs[rows64, pl.ds(256, 256)] = low
            dlhs[rows64, pl.ds(512, 256)] = high

        dxe[comp] = matmul(dlhs[...], der[...])

    def joined(rows64):
        return jnp.where(
            lane64 < 60, pltpu.roll(rx[3, rows64], 60, 1), pltpu.roll(rx[4, rows64], 120, 1)
        )

    received(0)
    received(3)
    gather((lambda r: rx[0, r], lambda r: rx[3, r]))
    pv[0] = matmul(inv[...], xr[...])
    derive(0)
    received(1)
    received(4)
    gather((lambda r: rx[1, r], joined))
    pv[1] = matmul(inv[...], xr[...])
    derive(1)
    received(2)
    gather((lambda r: rx[2, r], lambda r: rx[4, r]))
    pv[2, pl.ds(0, 512)] = matmul(inv[pl.ds(0, 512)], xr[...])

    def bases(comps):
        @pl.loop(0, 16)
        def _(block):
            at = pl.multiple_of(block * 32, 32)
            rows32 = pl.ds(at, 32)
            u, v, w = pv[0, rows32], pv[1, rows32], pv[2, rows32]
            first = u * rows[pl.ds(0, 1)] + v * rows[pl.ds(1, 1)]
            second = u * rows[pl.ds(2, 1)] + v * rows[pl.ds(3, 1)]
            if 0 in comps:
                uu[0, rows32] = u * rows[pl.ds(4, 1)] + v * rows[pl.ds(5, 1)]
                uu[1, rows32] = u * rows[pl.ds(6, 1)] + v * rows[pl.ds(7, 1)]
            layers = uu[0, rows32] + uu[1, rows32]
            for comp in comps:
                total = first * dxe[comp, rows32, pl.ds(0, 256)]
                total = total + second * dxe[comp, rows32, pl.ds(256, 256)]
                total = total + w * pv[comp, pl.ds(at + 512, 32)]
                base[comp, rows32] = total - layers * pv[comp, rows32]

    bases((0, 1))

    def send_back(index, source, target):
        pltpu.make_async_copy(source(me), target, recv2_sem.at[index]).start()

        @pl.loop(1, MODES)
        def _(k):
            to = lax.rem(me + k, MODES)
            pltpu.make_async_remote_copy(
                src_ref=source(to),
                dst_ref=target,
                send_sem=send2_sem.at[index],
                recv_sem=recv2_sem.at[index],
                device_id={"mode": to},
                device_id_type=MESH,
            ).start()

    def whole_back(group):
        send_back(
            group,
            lambda to: sb2.at[group, pl.ds(pl.multiple_of(to * LOCAL, LOCAL), LOCAL)],
            back.at[group, me],
        )

    def traces_on_planes(slot, load):
        @pl.loop(0, 8)
        def _(block):
            at = pl.multiple_of(block * 64, 64)
            high, low = halves(load(pl.ds(at, 64)))
            xa[pl.ds(at, 64)] = high
            xa[pl.ds(at + 512, 64)] = high
            xa[pl.ds(at + 1024, 64)] = low

        pa[slot] = matmul(inv[pl.ds(0, 512)], xa[...])

    def product(comp, loads_):
        count = len(loads_)

        @pl.loop(0, 8)
        def _(block):
            rows64 = pl.ds(pl.multiple_of(block * 64, 64), 64)
            for k, load in enumerate(loads_):
                high, low = halves(load(rows64))
                la[rows64, pl.ds(128 * k, 128)] = high
                la[rows64, pl.ds(128 * (count + k), 128)] = low

        wide = pl.ds(0, 256 * count)
        dxe[0] = matmul(la[:, wide], place[comp, wide])

        @pl.loop(0, 8)
        def _(block):
            at = pl.multiple_of(block * 64, 64)
            rows64 = pl.ds(at, 64)
            total = base[comp, rows64] + uu[0, rows64] * dxe[0, rows64, pl.ds(0, 256)]
            total = total + uu[1, rows64] * dxe[0, rows64, pl.ds(256, 256)]
            high, low = halves(total)
            xp[rows64] = high
            xp[pl.ds(at + 512, 64)] = high
            xp[pl.ds(at + 1024, 64)] = low

        result = matmul(fwd[...], xp[...])
        sb2[comp] = result[:, :128]
        tail[comp] = result[:, 128:]
        whole_back(comp)

    def half_tiles(k):
        tiles = rp[k][:, None]
        return jnp.concatenate([tiles, pltpu.roll(tiles, 64, 3)], axis=1).reshape(NZ, 128)

    received(6)
    rx[6] = half_tiles(0)
    traces_on_planes(0, lambda r: rx[6, r])
    product(0, (lambda r: pv[2, r, pl.ds(128, 128)], lambda r: pa[0, r]))
    received(5)
    traces_on_planes(1, lambda r: rx[5, r])
    product(1, (lambda r: pa[1, r],))
    lane512 = lax.broadcasted_iota(jnp.int32, (512, 128), 1)
    sb2[3] = jnp.where(lane512 < 68, tail[0], pltpu.roll(tail[1], 68, 1))
    whole_back(3)
    pv[2, pl.ds(512, 512)] = matmul(inv[pl.ds(512, 512)], xr[...])
    derive(2)
    bases((2,))
    received(7)
    received(8)
    low_rows = lax.broadcasted_iota(jnp.int32, (MODES, 8, 128), 1) < 4
    tiles = rp[2]
    pairs = []
    for even, odd in ((64, 32), (0, 96)):
        upper = pltpu.roll(pltpu.roll(tiles, odd, 2), 4, 1)
        lower = pltpu.roll(tiles, even, 2) if even else tiles
        pairs.append(jnp.where(low_rows, lower, upper)[:, None])
    quarter = jnp.concatenate(pairs, axis=1).reshape(NZ, 128)
    rx[6] = jnp.where(lane512 < 64, half_tiles(1), jnp.where(lane512 < 96, quarter, 0.0))
    traces_on_planes(0, lambda r: rx[6, r])
    product(2, (lambda r: pa[1, r], lambda r: pa[0, r]))
    lane3 = lax.broadcasted_iota(jnp.int32, (MODES, 8, 128), 2)
    ends = tail[2].reshape(MODES, 2, 8, 128)
    sh2[...] = jnp.where(lane3 < 64, ends[:, 0], pltpu.roll(ends[:, 1], 64, 2))
    send_back(4, lambda to: sh2.at[to], back_h.at[me])

    others1 = tail[1].reshape(MODES, 2, 8, 128)
    packed = None
    for k in (1, 0):
        end = jnp.where(lane3 < 4, pltpu.roll(ends[:, k], 64, 2), pltpu.roll(others1[:, k], 72, 2))
        for upper in (1, 0):
            block = 2 * k + upper
            moved = pltpu.roll(end, 4, 1) if upper else end
            moved = pltpu.roll(moved, 32 * block, 2) if block else moved
            packed = moved if packed is None else jnp.where(lane3 < 32 * block + 32, moved, packed)
    sq2[...] = packed
    few = pl.ds(0, 4)
    send_back(5, lambda to: sq2.at[to, few], back_q.at[me, few])

    leaving = []

    def leave(first, count):
        copy = pltpu.make_async_copy(
            done.at[pl.ds(first, count)], out.at[pl.ds(first, count)], out_sem.at[len(leaving)]
        )
        copy.start()
        leaving.append(copy)

    def arrived(index, ref):
        pltpu.make_async_copy(ref, ref, recv2_sem.at[index]).wait()

    for group, parts in (
        (0, ((0, 32),)),
        (1, ((49, 32),)),
        (3, ((32, 17), (81, 15))),
        (2, ((98, 32),)),
    ):
        arrived(group, back.at[group])

        @pl.loop(0, 2)
        def _(half):
            rows8 = pl.ds(pl.multiple_of(half * 8, 8), 8)

            def store(d, tile):
                done[RETURNS[group][d], rows8] = tile

            lane_swap(lambda p: back[group, p, rows8], store)

        for span in parts:
            leave(*span)

    def store_half(d, tile):
        done[HALF[d % 16], pl.ds(d // 16 * 8, 8)] = tile

    arrived(4, back_h)
    lane_swap(lambda p: back_h[p], store_half)
    leave(130, 16)

    def store_last(d, tile):
        if d % 8 < len(QUARTER):
            done[QUARTER[d % 8], pl.ds(d // 8 * 4, 4)] = tile[:4]

    arrived(5, back_q.at[:, few])
    lane_swap(lambda p: back_q[p], store_last)
    leave(96, 2)
    leave(146, 1)

    @pl.when(has_above)
    def _():
        halo[0].wait_send()

    @pl.when(has_below)
    def _():
        halo[1].wait_send()

    for group in range(GROUPS):
        sent = sb.at[group, pl.ds(0, MODES - 1)]
        pltpu.make_async_copy(sent, sent, send_sem.at[group]).wait()
    for k in range(3):
        sent = sp.at[k, pl.ds(0, MODES - 1), part_rows(GROUPS + k)]
        pltpu.make_async_copy(sent, sent, send_sem.at[GROUPS + k]).wait()
    for group in range(4):
        sent = sb2.at[group, pl.ds(0, (MODES - 1) * LOCAL)]
        pltpu.make_async_copy(sent, sent, send2_sem.at[group]).wait()
    sent = sh2.at[pl.ds(0, MODES - 1)]
    pltpu.make_async_copy(sent, sent, send2_sem.at[4]).wait()
    sent = sq2.at[pl.ds(0, MODES - 1), few]
    pltpu.make_async_copy(sent, sent, send2_sem.at[5]).wait()
    for copy in leaving:
        copy.wait()


def shards(velocity, metric_terms, lift_scale, neighbour, neighbour_side, orientation):
    v = jnp.transpose(velocity, (0, 2, 1, 3)).reshape(3 * NN, LOCAL, ELEMS)
    metric = jnp.transpose(metric_terms, (1, 0, 2))
    lift = jnp.transpose(lift_scale, (0, 2, 1, 3)).reshape(2 * NP, 4, ELEMS)
    operands = [v, metric, lift, neighbour, neighbour_side, orientation]
    operands += [jnp.asarray(t) for t in tables()]
    anywhere = pl.BlockSpec(memory_space=pl.ANY)
    vmem = pltpu.VMEM
    dma = pltpu.SemaphoreType.DMA
    out = pl.pallas_call(
        main_kernel,
        out_shape=pltpu.VMEM((3 * NN, LOCAL, ELEMS), F32),
        in_specs=[anywhere] * 10,
        out_specs=anywhere,
        scratch_shapes=[
            vmem((4, MODES, LOCAL, 128), F32),
            vmem((MODES, 8, 128), F32),
            vmem((MODES, 8, 128), F32),
            vmem((3 * NN, LOCAL, 128), F32),
            vmem((3 * NN, LOCAL, 128), F32),
            vmem((GROUPS, 32, LOCAL, 128), F32),
            vmem((3, 32, 8, 128), F32),
            vmem((GROUPS, MODES, LOCAL, 128), F32),
            vmem((3, MODES, 8, 128), F32),
            vmem((GROUPS + 1, NZ, 128), F32),
            vmem((3, MODES, 8, 128), F32),
            vmem((4, NZ, 128), F32),
            vmem((MODES, 8, 128), F32),
            vmem((MODES, 8, 128), F32),
            vmem((2 * NZ, 3 * NZ), BF16),
            vmem((NZ, 3 * NZ), BF16),
            vmem((768, 512), BF16),
            vmem((3, 512, 512), BF16),
            vmem((NN, 8, 128), F32),
            vmem((2 * NP, 8, 128), F32),
            vmem((8, 128), jnp.int32),
            vmem((8, 128), jnp.int32),
            vmem((8, 128), jnp.int32),
            vmem((3, 224, 512), BF16),
            vmem((32, 512), BF16),
            vmem((512, 512), BF16),
            vmem((128, 512), BF16),
            vmem((512, 128), BF16),
            vmem((112, 128), F32),
            vmem((112, 128), F32),
            vmem((112, 128), F32),
            vmem((112, 128), F32),
            vmem((8, 256), F32),
            vmem((3 * NZ, 256), BF16),
            vmem((3, 2 * NZ, 256), F32),
            vmem((NZ, 768), BF16),
            vmem((3, NZ, 512), F32),
            vmem((3, NZ, 256), F32),
            vmem((2, NZ, 256), F32),
            vmem((3 * NZ, 128), BF16),
            vmem((2, NZ, 128), F32),
            vmem((NZ, 512), BF16),
            vmem((3 * NZ, 256), BF16),
            vmem((3, NZ, 128), F32),
            dma((len(PIECES),)),
            dma((10,)),
            dma((GROUPS + 3,)),
            dma((GROUPS + 3,)),
            dma((6,)),
            dma((6,)),
            dma((2,)),
            dma((2,)),
            dma((8,)),
            pltpu.SemaphoreType.REGULAR,
        ],
        compiler_params=pltpu.CompilerParams(
            collective_id=0, has_side_effects=True, vmem_limit_bytes=48 << 20
        ),
        name="advect",
    )(*[pltpu.with_memory_space_constraint(x, pltpu.HBM) for x in operands])
    index = lax.axis_index("mode") * LOCAL + jnp.arange(LOCAL, dtype=jnp.int32)
    weighting = jnp.where(index < 2, 1.0 / NZ, 2.0 / NZ).astype(F32)
    out = out.reshape(3, NN, LOCAL, ELEMS) * weighting[:, None]
    return jnp.transpose(out, (0, 2, 1, 3))


def solution(mesh):
    return jax.shard_map(
        shards,
        mesh=mesh,
        in_specs=(
            P(None, "mode", None, "plane"),
            P(None, None, "plane"),
            P(None, None, None, "plane"),
            P(None, "plane"),
            P(None, "plane"),
            P(None, "plane"),
        ),
        out_specs=P(None, "mode", None, "plane"),
        check_vma=False,
    )
```

```python
import jax
import jax.numpy as jnp
import ml_dtypes
import numpy as np
from jax import lax
from jax.experimental import pallas as pl
from jax.experimental.pallas import tpu as pltpu
from jax.sharding import PartitionSpec as P

MESH = pl.DeviceIdType.MESH
F32 = jnp.float32
BF16 = jnp.bfloat16

NP = 7
NN = 49
NZ = 512
MODES = 32
PLANES = 8
LOCAL = 16
ELEMS = 128
SPAN_WAVENUMBER = 0.25
GROUPS = 6

GLL_POINTS = (
    -1.0,
    -0.830223896278567,
    -0.468848793470714,
    0.0,
    0.468848793470714,
    0.830223896278567,
    1.0,
)

PIECES = (
    (0, 0, 0, 32),
    (3, 0, 32, 17),
    (3, 17, 81, 15),
    (1, 0, 49, 32),
    (4, 0, 130, 17),
    (4, 17, 96, 2),
    (2, 0, 98, 32),
)
TRACES = (
    (0, 0, 13, 4, 19),
    (0, 13, 15, 6, 0),
    (1, 0, 28, 5, 0),
    (2, 0, 4, 5, 28),
    (2, 4, 16, 7, 0),
    (2, 20, 8, 8, 0),
)
RETURNS = (
    tuple(range(0, 32)),
    tuple(range(49, 81)),
    tuple(range(98, 130)),
    tuple(range(32, 49)) + tuple(range(81, 96)),
)
HALF = tuple(range(130, 146))
QUARTER = (146, 96, 97)


def derivative_matrix():
    points = np.array(GLL_POINTS)
    identity = np.eye(NP)
    offdiag = points[:, None] - points[None, :] + identity
    weights = 1.0 / np.prod(offdiag, axis=1)
    matrix = weights[None, :] / weights[:, None] / offdiag
    matrix = matrix * (1.0 - identity)
    return matrix - identity * matrix.sum(axis=1)[:, None]


def split_np(table):
    table = table.astype(np.float32)
    high = table.astype(ml_dtypes.bfloat16)
    low = (table - high.astype(np.float32)).astype(ml_dtypes.bfloat16)
    return high, low


def side_node(side, position):
    return (position, position * NP + NP - 1, (NP - 1) * NP + position, position * NP)[side]


def tables():
    index = np.arange(NZ)
    wave = np.where(index == 1, NZ // 2, index // 2)
    phase = (wave[:, None] * index[None, :] % NZ) * (2.0 * np.pi / NZ)
    sine_row = ((index % 2 == 1) & (index > 1))[:, None]
    inverse = np.where(sine_row, np.sin(phase), np.cos(phase))
    slope = np.where(index < 2, 0.0, wave)[:, None] * SPAN_WAVENUMBER
    slope = slope * np.where(sine_row, np.cos(phase), -np.sin(phase))
    high, low = split_np(np.concatenate([inverse.T, slope.T], axis=0))
    backward = np.concatenate([high, low, high], axis=1)
    high, low = split_np(inverse)
    forward = np.concatenate([high, low, high], axis=1)
    matrix = derivative_matrix()
    derive = np.zeros((256, 512))
    for j in range(NP):
        for i in range(NP):
            for b in range(NP):
                for e in range(4):
                    derive[4 * (j * NP + b) + e, 4 * (j * NP + i) + e] = matrix[i, b]
                    derive[4 * (b * NP + i) + e, 256 + 4 * (j * NP + i) + e] = matrix[j, b]
    high, low = split_np(derive)
    derive = np.concatenate([high, high, low], axis=0)
    place = np.zeros((3, 256, 512))
    starts = {(0, 0): 76, (0, 13): 128, (1, 0): 0, (2, 0): 112, (2, 4): 128, (2, 20): 192}
    for comp, first, count, _, _ in TRACES:
        for k in range(count):
            side, position = divmod(first + k, NP)
            for e in range(4):
                column = 256 * (side % 2) + 4 * side_node(side, position) + e
                place[comp, starts[comp, first] + 4 * k + e, column] = 1.0
    place = place.astype(ml_dtypes.bfloat16)
    place[1, 128:] = place[1, :128]
    return backward, forward, derive, np.concatenate([place, place], axis=1)


def halves(value):
    high = value.astype(BF16)
    return high, (value - high.astype(F32)).astype(BF16)


def lane_swap(load, store):
    lane = lax.broadcasted_iota(jnp.int32, (8, 128), 1)
    tiles = [None] * 32
    for p in range(32):
        tiles[-p % 32] = pltpu.roll(load(p), 4 * p, 1) if p else load(p)
    for bit in range(5):
        mask = (lane & (4 << bit)) != 0
        tiles = [jnp.where(mask, tiles[(j - (1 << bit)) % 32], tiles[j]) for j in range(32)]
    for d in range(32):
        store(d, pltpu.roll(tiles[d], 128 - 4 * d, 1) if d else tiles[d])


def matmul(a, b):
    return jnp.dot(a, b, preferred_element_type=F32)


def matmul_nt(a, b):
    return lax.dot_general(a, b, (((1,), (1,)), ((), ())), preferred_element_type=F32)


def exact(a, b):
    return jnp.dot(a, b, precision=lax.Precision.HIGHEST, preferred_element_type=F32)


def main_kernel(
    v_hbm,
    metric_hbm,
    lift_hbm,
    nb_hbm,
    ns_hbm,
    or_hbm,
    inv_hbm,
    fwd_hbm,
    der_hbm,
    place_hbm,
    done,
    back,
    back_h,
    back_q,
    vn,
    vs,
    vp,
    sb,
    sp,
    rx,
    rp,
    sb2,
    sh2,
    sq2,
    inv,
    fwd,
    der,
    place,
    met,
    lif,
    nbv,
    nsv,
    orv,
    lmat,
    kmat,
    oh,
    sel,
    oht,
    up_out,
    dn_out,
    up_in,
    dn_in,
    rows,
    xr,
    pv,
    dlhs,
    dxe,
    base,
    uu,
    xa,
    pa,
    la,
    xp,
    tail,
    load_sem,
    in_sem,
    send_sem,
    recv_sem,
    send2_sem,
    recv2_sem,
    halo_send,
    halo_recv,
    ready_sem,
):
    me = lax.axis_index("mode")
    part = lax.axis_index("plane")
    has_above = part < PLANES - 1
    has_below = part > 0
    above = lax.rem(part + 1, PLANES)
    below = lax.rem(part + PLANES - 1, PLANES)

    barrier = pltpu.get_barrier_semaphore()

    @pl.loop(1, MODES, unroll=True)
    def _(k):
        pl.semaphore_signal(
            barrier, inc=1, device_id={"mode": lax.rem(me + k, MODES)}, device_id_type=MESH
        )

    @pl.when(has_above)
    def _():
        pl.semaphore_signal(barrier, inc=1, device_id={"plane": above}, device_id_type=MESH)

    def entered():
        @pl.when(has_below)
        def _():
            pl.semaphore_wait(barrier, MODES)
            pl.semaphore_signal(ready_sem, inc=1, device_id={"plane": below}, device_id_type=MESH)

        @pl.when(part == 0)
        def _():
            pl.semaphore_wait(barrier, MODES - 1)

    nbv[...] = jnp.full((8, 128), -1, jnp.int32)
    nsv[...] = jnp.zeros((8, 128), jnp.int32)
    orv[...] = jnp.zeros((8, 128), jnp.int32)
    met[...] = jnp.zeros_like(met)
    lif[...] = jnp.zeros_like(lif)
    loads = []
    for k, (group, slot, row, count) in enumerate(PIECES):
        copy = pltpu.make_async_copy(
            v_hbm.at[pl.ds(row, count)], vs.at[group, pl.ds(slot, count)], load_sem.at[k]
        )
        copy.start()
        loads.append((group, copy))
    others = []
    for k, (src, dst) in enumerate(
        (
            (v_hbm, vn),
            (nb_hbm, nbv.at[pl.ds(0, 4)]),
            (ns_hbm, nsv.at[pl.ds(0, 4)]),
            (or_hbm, orv.at[pl.ds(0, 4)]),
            (metric_hbm, met.at[:, pl.ds(0, 4)]),
            (lift_hbm, lif.at[:, pl.ds(0, 4)]),
            (inv_hbm, inv),
            (der_hbm, der),
            (place_hbm, place),
            (fwd_hbm, fwd),
        )
    ):
        copy = pltpu.make_async_copy(src, dst, in_sem.at[k])
        copy.start()
        others.append(copy)

    vp[...] = jnp.zeros_like(vp)

    @pl.when(part == 0)
    def _():
        up_in[...] = jnp.zeros_like(up_in)

    @pl.when(part == PLANES - 1)
    def _():
        dn_in[...] = jnp.zeros_like(dn_in)

    def scatter(group):
        @pl.loop(0, 2)
        def _(half):
            rows8 = pl.ds(pl.multiple_of(half * 8, 8), 8)

            def store(d, tile):
                sb[group, d, rows8] = tile

            lane_swap(lambda p: vs[group, p, rows8], store)

    def send(group):
        mine = rx.at[group, pl.ds(pl.multiple_of(me * LOCAL, LOCAL), LOCAL)]
        pltpu.make_async_copy(sb.at[group, me], mine, recv_sem.at[group]).start()

        @pl.loop(1, MODES)
        def _(k):
            to = lax.rem(me + k, MODES)
            pltpu.make_async_remote_copy(
                src_ref=sb.at[group, to],
                dst_ref=mine,
                send_sem=send_sem.at[group],
                recv_sem=recv_sem.at[group],
                device_id={"mode": to},
                device_id_type=MESH,
            ).start()

    def depart(group):
        for owner, copy in loads:
            if owner == group:
                copy.wait()
        scatter(group)
        if group == 0:
            entered()
        send(group)

    def part_rows(group):
        return pl.ds(0, 4 if group == 8 else 8)

    def depart_part(group):
        k = group - GROUPS

        def store(d, tile):
            sp[k, d] = tile

        lane_swap(lambda p: vp[k, p], store)
        some = part_rows(group)
        pltpu.make_async_copy(sp.at[k, me, some], rp.at[k, me, some], recv_sem.at[group]).start()

        @pl.loop(1, MODES)
        def _(j):
            to = lax.rem(me + j, MODES)
            pltpu.make_async_remote_copy(
                src_ref=sp.at[k, to, some],
                dst_ref=rp.at[k, me, some],
                send_sem=send_sem.at[group],
                recv_sem=recv_sem.at[group],
                device_id={"mode": to},
                device_id_type=MESH,
            ).start()

    for group in (0, 3, 1):
        depart(group)

    for copy in others[:4]:
        copy.wait()
    nb = nbv[...]
    exists = nb >= 0
    owner = lax.shift_right_arithmetic(nb, 7)
    target = nsv[...] * ELEMS + (nb & (ELEMS - 1))
    own_key = jnp.where(exists & (owner == part), target, -1)
    is_up = exists & (owner == part + 1)
    is_dn = exists & (owner == part - 1)
    strict = (
        lax.broadcasted_iota(jnp.int32, (128, 128), 0)
        < lax.broadcasted_iota(jnp.int32, (128, 128), 1)
    ).astype(F32)
    ranks = []
    for border in (is_up, is_dn):
        flag = jnp.where(border, 1.0, 0.0)
        before = exact(flag, strict)
        totals = jnp.sum(flag, axis=1, keepdims=True)
        offset = jnp.zeros((1, 1), F32)
        found = []
        for side in range(4):
            found.append(before[side : side + 1] + offset)
            offset = offset + totals[side : side + 1]
        ranks.append(found)
    row128 = lax.broadcasted_iota(jnp.int32, (128, 128), 0).astype(F32)
    row512 = lax.broadcasted_iota(jnp.int32, (512, 128), 0)
    for side in range(4):
        lanes = pl.ds(side * 128, 128)
        one = slice(side, side + 1)
        slot = jnp.where(
            is_up[one], ranks[0][side], jnp.where(is_dn[one], 32.0 + ranks[1][side], -1.0)
        )
        sel[:, lanes] = jnp.where(row128 == slot, 1.0, 0.0).astype(BF16)
        oh[:, lanes] = jnp.where(row512 == own_key[one], 1.0, 0.0).astype(BF16)
        high, low = halves(jnp.broadcast_to((target[one] + 1).astype(F32), (16, 128)))
        kmat[pl.ds(0, 16), lanes] = high
        kmat[pl.ds(16, 16), lanes] = low
    turned = orv[...] == 1

    @pl.loop(0, 3)
    def _(comp):
        for position in range(NP):
            for side in range(4):
                straight = vn[comp * NN + side_node(side, position)]
                reverse = vn[comp * NN + side_node(side, NP - 1 - position)]
                value = jnp.where(turned[side : side + 1], reverse, straight)
                high, low = halves(value)
                lanes = pl.ds(side * 128, 128)
                lmat[comp, pl.ds(position * 16, 16), lanes] = high
                lmat[comp, pl.ds(112 + position * 16, 16), lanes] = low

    picked = []
    for comp in range(3):
        both = matmul_nt(lmat[comp], sel[...])
        picked.append(both[:112] + both[112:])
    both = matmul_nt(kmat[...], sel[...])
    keys = jnp.concatenate([both[:16] + both[16:], jnp.zeros((96, 128), F32)], axis=0)
    picked.append(keys)
    lane = lax.broadcasted_iota(jnp.int32, (112, 128), 1)
    for ref, shift in ((up_out, 0), (dn_out, 96)):
        packed = None
        for k in (3, 2, 1, 0):
            by = (32 * k + shift) % 128
            moved = pltpu.roll(picked[k], by, 1) if by else picked[k]
            packed = moved if packed is None else jnp.where(lane < 32 * k + 32, moved, packed)
        ref[...] = packed
    halo = [
        pltpu.make_async_remote_copy(
            src_ref=src,
            dst_ref=dst,
            send_sem=halo_send.at[k],
            recv_sem=halo_recv.at[k],
            device_id={"plane": to},
            device_id_type=MESH,
        )
        for k, (src, dst, to) in enumerate(((up_out, up_in, above), (dn_out, dn_in, below)))
    ]

    @pl.when(has_below)
    def _():
        halo[1].start()

    @pl.when(has_above)
    def _():
        pl.semaphore_wait(ready_sem, 1)
        halo[0].start()

    for copy in others[4:6]:
        copy.wait()
    fold = (
        lax.broadcasted_iota(jnp.int32, (128, 256), 0)
        == 4 * me + (lax.broadcasted_iota(jnp.int32, (128, 256), 1) & 3)
    ).astype(F32)
    spread = exact(met[...].reshape(NN * 8, 128), fold).reshape(NN, 8, 256)
    node3 = lax.shift_right_arithmetic(lax.broadcasted_iota(jnp.int32, (NN, 8, 256), 2), 2)
    here = node3 == lax.broadcasted_iota(jnp.int32, (NN, 8, 256), 0)
    metric_rows = jnp.sum(jnp.where(here, spread, 0.0), axis=0)
    rows[pl.ds(0, 4)] = metric_rows[:4]
    live = exact(jnp.where(exists, 0.5, 0.0), fold)
    spread = exact(lif[...].reshape(2 * NP * 8, 128), fold).reshape(2 * NP, 8, 256)
    node2 = lax.shift_right_arithmetic(lax.broadcasted_iota(jnp.int32, (8, 256), 1), 2)
    side2 = lax.broadcasted_iota(jnp.int32, (8, 256), 0)
    for axis in range(2):
        total = jnp.zeros((8, 256), F32)
        for position in range(NP):
            wanted = jnp.full((8, 256), -1, jnp.int32)
            for side in range(4):
                wanted = jnp.where(side2 == side, side_node(side, position), wanted)
            total = total + jnp.where(node2 == wanted, spread[axis * NP + position], 0.0)
        total = total * live
        rows[pl.ds(4 + axis, 1)] = total[0:1] + total[2:3]
        rows[pl.ds(6 + axis, 1)] = total[1:2] + total[3:4]

    @pl.when(has_below)
    def _():
        halo[0].wait_recv()

    @pl.when(has_above)
    def _():
        halo[1].wait_recv()

    lane1 = lax.broadcasted_iota(jnp.int32, (8, 128), 1)
    key_up = pltpu.roll(up_in[pl.ds(0, 8)], 32, 1)
    key_dn = pltpu.roll(dn_in[pl.ds(0, 8)], 64, 1)
    key = jnp.where(lane1 < 32, key_up, jnp.where(lane1 < 64, key_dn, 0.0))[0:1]
    oht[...] = jnp.where((row512 + 1).astype(F32) == key, 1.0, 0.0).astype(BF16)
    for comp in range(3):
        both = matmul(lmat[comp], oh[...])
        across = both[:112] + both[112:]
        from_up = pltpu.roll(up_in[...], (128 - 32 * comp) % 128, 1) if comp else up_in[...]
        from_dn = pltpu.roll(dn_in[...], (160 - 32 * comp) % 128, 1) if comp != 1 else dn_in[...]
        high, low = halves(jnp.where(lane < 32, from_up, jnp.where(lane < 64, from_dn, 0.0)))
        both = matmul_nt(jnp.concatenate([high, low], axis=0), oht[...])
        across = across + (both[:112] + both[112:])
        for owner, first, count, group, slot in TRACES:
            if owner != comp:
                continue
            for k in range(count):
                side, position = divmod(first + k, NP)
                lanes = slice(side * 128, side * 128 + 128)
                where = slice(position * 16, position * 16 + 16)
                if group < GROUPS:
                    vs[group, slot + k] = across[where, lanes]
                    continue
                parts = 4 if group == 8 else 2
                for part_at in range(parts):
                    size = 16 // parts
                    at = position * 16 + part_at * size
                    vp[group - GROUPS, part_at * (32 // parts) + k, pl.ds(0, size)] = across[
                        at : at + size, lanes
                    ]
        if comp == 0:
            depart(4)
            depart(2)
            depart_part(6)
        elif comp == 1:
            continue
        else:
            depart(5)
            depart_part(7)
            depart_part(8)

    def received(group):
        ref = rx.at[group] if group < GROUPS else rp.at[group - GROUPS, :, part_rows(group)]
        pltpu.make_async_copy(ref, ref, recv_sem.at[group]).wait()

    for copy in others[6:]:
        copy.wait()
    lane64 = lax.broadcasted_iota(jnp.int32, (64, 128), 1)

    def gather(pieces):
        @pl.loop(0, 8)
        def _(block):
            at = pl.multiple_of(block * 64, 64)
            for k in range(2):
                high, low = halves(pieces[k](pl.ds(at, 64)))
                lanes = pl.ds(k * 128, 128)
                xr[pl.ds(at, 64), lanes] = high
                xr[pl.ds(at + 512, 64), lanes] = high
                xr[pl.ds(at + 1024, 64), lanes] = low

    def derive(comp):
        @pl.loop(0, 8)
        def _(block):
            rows64 = pl.ds(pl.multiple_of(block * 64, 64), 64)
            high, low = halves(pv[comp, rows64])
            dlhs[rows64, pl.ds(0, 256)] = high
            dlhs[rows64, pl.ds(256, 256)] = low
            dlhs[rows64, pl.ds(512, 256)] = high

        dxe[comp] = matmul(dlhs[...], der[...])

    def joined(rows64):
        return jnp.where(
            lane64 < 60, pltpu.roll(rx[3, rows64], 60, 1), pltpu.roll(rx[4, rows64], 120, 1)
        )

    received(0)
    received(3)
    gather((lambda r: rx[0, r], lambda r: rx[3, r]))
    pv[0] = matmul(inv[...], xr[...])
    derive(0)
    received(1)
    received(4)
    gather((lambda r: rx[1, r], joined))
    pv[1] = matmul(inv[...], xr[...])
    derive(1)
    received(2)
    gather((lambda r: rx[2, r], lambda r: rx[4, r]))
    pv[2, pl.ds(0, 512)] = matmul(inv[pl.ds(0, 512)], xr[...])

    def bases(comps):
        @pl.loop(0, 16)
        def _(block):
            at = pl.multiple_of(block * 32, 32)
            rows32 = pl.ds(at, 32)
            u, v, w = pv[0, rows32], pv[1, rows32], pv[2, rows32]
            first = u * rows[pl.ds(0, 1)] + v * rows[pl.ds(1, 1)]
            second = u * rows[pl.ds(2, 1)] + v * rows[pl.ds(3, 1)]
            if 0 in comps:
                uu[0, rows32] = u * rows[pl.ds(4, 1)] + v * rows[pl.ds(5, 1)]
                uu[1, rows32] = u * rows[pl.ds(6, 1)] + v * rows[pl.ds(7, 1)]
            layers = uu[0, rows32] + uu[1, rows32]
            for comp in comps:
                total = first * dxe[comp, rows32, pl.ds(0, 256)]
                total = total + second * dxe[comp, rows32, pl.ds(256, 256)]
                total = total + w * pv[comp, pl.ds(at + 512, 32)]
                base[comp, rows32] = total - layers * pv[comp, rows32]

    bases((0, 1))

    def send_back(index, source, target):
        pltpu.make_async_copy(source(me), target, recv2_sem.at[index]).start()

        @pl.loop(1, MODES, unroll=True)
        def _(k):
            to = lax.rem(me + k, MODES)
            pltpu.make_async_remote_copy(
                src_ref=source(to),
                dst_ref=target,
                send_sem=send2_sem.at[index],
                recv_sem=recv2_sem.at[index],
                device_id={"mode": to},
                device_id_type=MESH,
            ).start()

    def whole_back(group):
        send_back(
            group,
            lambda to: sb2.at[group, pl.ds(pl.multiple_of(to * LOCAL, LOCAL), LOCAL)],
            back.at[group, me],
        )

    def traces_on_planes(slot, load):
        @pl.loop(0, 8)
        def _(block):
            at = pl.multiple_of(block * 64, 64)
            high, low = halves(load(pl.ds(at, 64)))
            xa[pl.ds(at, 64)] = high
            xa[pl.ds(at + 512, 64)] = high
            xa[pl.ds(at + 1024, 64)] = low

        pa[slot] = matmul(inv[pl.ds(0, 512)], xa[...])

    def product(comp, loads_):
        count = len(loads_)

        @pl.loop(0, 8)
        def _(block):
            rows64 = pl.ds(pl.multiple_of(block * 64, 64), 64)
            for k, load in enumerate(loads_):
                high, low = halves(load(rows64))
                la[rows64, pl.ds(128 * k, 128)] = high
                la[rows64, pl.ds(128 * (count + k), 128)] = low

        wide = pl.ds(0, 256 * count)
        dxe[0] = matmul(la[:, wide], place[comp, wide])

        @pl.loop(0, 8)
        def _(block):
            at = pl.multiple_of(block * 64, 64)
            rows64 = pl.ds(at, 64)
            total = base[comp, rows64] + uu[0, rows64] * dxe[0, rows64, pl.ds(0, 256)]
            total = total + uu[1, rows64] * dxe[0, rows64, pl.ds(256, 256)]
            high, low = halves(total)
            xp[rows64] = high
            xp[pl.ds(at + 512, 64)] = high
            xp[pl.ds(at + 1024, 64)] = low

        result = matmul(fwd[...], xp[...])
        sb2[comp] = result[:, :128]
        tail[comp] = result[:, 128:]
        whole_back(comp)

    def half_tiles(k):
        tiles = rp[k][:, None]
        return jnp.concatenate([tiles, pltpu.roll(tiles, 64, 3)], axis=1).reshape(NZ, 128)

    received(6)
    rx[6] = half_tiles(0)
    traces_on_planes(0, lambda r: rx[6, r])
    product(0, (lambda r: pv[2, r, pl.ds(128, 128)], lambda r: pa[0, r]))
    received(5)
    traces_on_planes(1, lambda r: rx[5, r])
    product(1, (lambda r: pa[1, r],))
    lane512 = lax.broadcasted_iota(jnp.int32, (512, 128), 1)
    sb2[3] = jnp.where(lane512 < 68, tail[0], pltpu.roll(tail[1], 68, 1))
    whole_back(3)
    pv[2, pl.ds(512, 512)] = matmul(inv[pl.ds(512, 512)], xr[...])
    derive(2)
    bases((2,))
    received(7)
    received(8)
    low_rows = lax.broadcasted_iota(jnp.int32, (MODES, 8, 128), 1) < 4
    tiles = rp[2]
    pairs = []
    for even, odd in ((64, 32), (0, 96)):
        upper = pltpu.roll(pltpu.roll(tiles, odd, 2), 4, 1)
        lower = pltpu.roll(tiles, even, 2) if even else tiles
        pairs.append(jnp.where(low_rows, lower, upper)[:, None])
    quarter = jnp.concatenate(pairs, axis=1).reshape(NZ, 128)
    rx[6] = jnp.where(lane512 < 64, half_tiles(1), jnp.where(lane512 < 96, quarter, 0.0))
    traces_on_planes(0, lambda r: rx[6, r])
    product(2, (lambda r: pa[1, r], lambda r: pa[0, r]))
    lane3 = lax.broadcasted_iota(jnp.int32, (MODES, 8, 128), 2)
    ends = tail[2].reshape(MODES, 2, 8, 128)
    sh2[...] = jnp.where(lane3 < 64, ends[:, 0], pltpu.roll(ends[:, 1], 64, 2))
    send_back(4, lambda to: sh2.at[to], back_h.at[me])

    others1 = tail[1].reshape(MODES, 2, 8, 128)
    packed = None
    for k in (1, 0):
        end = jnp.where(lane3 < 4, pltpu.roll(ends[:, k], 64, 2), pltpu.roll(others1[:, k], 72, 2))
        for upper in (1, 0):
            block = 2 * k + upper
            moved = pltpu.roll(end, 4, 1) if upper else end
            moved = pltpu.roll(moved, 32 * block, 2) if block else moved
            packed = moved if packed is None else jnp.where(lane3 < 32 * block + 32, moved, packed)
    sq2[...] = packed
    few = pl.ds(0, 4)
    send_back(5, lambda to: sq2.at[to, few], back_q.at[me, few])

    def arrived(index, ref):
        pltpu.make_async_copy(ref, ref, recv2_sem.at[index]).wait()

    for group in (0, 1, 3, 2):
        arrived(group, back.at[group])

        @pl.loop(0, 2)
        def _(half):
            rows8 = pl.ds(pl.multiple_of(half * 8, 8), 8)

            def store(d, tile):
                done[RETURNS[group][d], rows8] = tile

            lane_swap(lambda p: back[group, p, rows8], store)

    def store_half(d, tile):
        done[HALF[d % 16], pl.ds(d // 16 * 8, 8)] = tile

    arrived(4, back_h)
    lane_swap(lambda p: back_h[p], store_half)

    def store_last(d, tile):
        if d % 8 < len(QUARTER):
            done[QUARTER[d % 8], pl.ds(d // 8 * 4, 4)] = tile[:4]

    arrived(5, back_q.at[:, few])
    lane_swap(lambda p: back_q[p], store_last)

    @pl.when(has_above)
    def _():
        halo[0].wait_send()

    @pl.when(has_below)
    def _():
        halo[1].wait_send()

    for group in range(GROUPS):
        sent = sb.at[group, pl.ds(0, MODES - 1)]
        pltpu.make_async_copy(sent, sent, send_sem.at[group]).wait()
    for k in range(3):
        sent = sp.at[k, pl.ds(0, MODES - 1), part_rows(GROUPS + k)]
        pltpu.make_async_copy(sent, sent, send_sem.at[GROUPS + k]).wait()
    for group in range(4):
        sent = sb2.at[group, pl.ds(0, (MODES - 1) * LOCAL)]
        pltpu.make_async_copy(sent, sent, send2_sem.at[group]).wait()
    sent = sh2.at[pl.ds(0, MODES - 1)]
    pltpu.make_async_copy(sent, sent, send2_sem.at[4]).wait()
    sent = sq2.at[pl.ds(0, MODES - 1), few]
    pltpu.make_async_copy(sent, sent, send2_sem.at[5]).wait()


def shards(velocity, metric_terms, lift_scale, neighbour, neighbour_side, orientation):
    v = jnp.transpose(velocity, (0, 2, 1, 3)).reshape(3 * NN, LOCAL, ELEMS)
    metric = jnp.transpose(metric_terms, (1, 0, 2))
    lift = jnp.transpose(lift_scale, (0, 2, 1, 3)).reshape(2 * NP, 4, ELEMS)
    operands = [v, metric, lift, neighbour, neighbour_side, orientation]
    operands += [jnp.asarray(t) for t in tables()]
    anywhere = pl.BlockSpec(memory_space=pl.ANY)
    vmem = pltpu.VMEM
    dma = pltpu.SemaphoreType.DMA
    out = pl.pallas_call(
        main_kernel,
        out_shape=pltpu.VMEM((3 * NN, LOCAL, ELEMS), F32),
        in_specs=[anywhere] * 10,
        out_specs=pl.BlockSpec(memory_space=vmem),
        scratch_shapes=[
            vmem((4, MODES, LOCAL, 128), F32),
            vmem((MODES, 8, 128), F32),
            vmem((MODES, 8, 128), F32),
            vmem((3 * NN, LOCAL, 128), F32),
            vmem((GROUPS, 32, LOCAL, 128), F32),
            vmem((3, 32, 8, 128), F32),
            vmem((GROUPS, MODES, LOCAL, 128), F32),
            vmem((3, MODES, 8, 128), F32),
            vmem((GROUPS + 1, NZ, 128), F32),
            vmem((3, MODES, 8, 128), F32),
            vmem((4, NZ, 128), F32),
            vmem((MODES, 8, 128), F32),
            vmem((MODES, 8, 128), F32),
            vmem((2 * NZ, 3 * NZ), BF16),
            vmem((NZ, 3 * NZ), BF16),
            vmem((768, 512), BF16),
            vmem((3, 512, 512), BF16),
            vmem((NN, 8, 128), F32),
            vmem((2 * NP, 8, 128), F32),
            vmem((8, 128), jnp.int32),
            vmem((8, 128), jnp.int32),
            vmem((8, 128), jnp.int32),
            vmem((3, 224, 512), BF16),
            vmem((32, 512), BF16),
            vmem((512, 512), BF16),
            vmem((128, 512), BF16),
            vmem((512, 128), BF16),
            vmem((112, 128), F32),
            vmem((112, 128), F32),
            vmem((112, 128), F32),
            vmem((112, 128), F32),
            vmem((8, 256), F32),
            vmem((3 * NZ, 256), BF16),
            vmem((3, 2 * NZ, 256), F32),
            vmem((NZ, 768), BF16),
            vmem((3, NZ, 512), F32),
            vmem((3, NZ, 256), F32),
            vmem((2, NZ, 256), F32),
            vmem((3 * NZ, 128), BF16),
            vmem((2, NZ, 128), F32),
            vmem((NZ, 512), BF16),
            vmem((3 * NZ, 256), BF16),
            vmem((3, NZ, 128), F32),
            dma((len(PIECES),)),
            dma((10,)),
            dma((GROUPS + 3,)),
            dma((GROUPS + 3,)),
            dma((6,)),
            dma((6,)),
            dma((2,)),
            dma((2,)),
            pltpu.SemaphoreType.REGULAR,
        ],
        compiler_params=pltpu.CompilerParams(
            collective_id=0, has_side_effects=True, vmem_limit_bytes=48 << 20
        ),
        name="advect",
    )(*[pltpu.with_memory_space_constraint(x, pltpu.HBM) for x in operands])
    index = lax.axis_index("mode") * LOCAL + jnp.arange(LOCAL, dtype=jnp.int32)
    weighting = jnp.where(index < 2, 1.0 / NZ, 2.0 / NZ).astype(F32)
    out = out.reshape(3, NN, LOCAL, ELEMS) * weighting[:, None]
    return jnp.transpose(out, (0, 2, 1, 3))


def solution(mesh):
    return jax.shard_map(
        shards,
        mesh=mesh,
        in_specs=(
            P(None, "mode", None, "plane"),
            P(None, None, "plane"),
            P(None, None, None, "plane"),
            P(None, "plane"),
            P(None, "plane"),
            P(None, "plane"),
        ),
        out_specs=P(None, "mode", None, "plane"),
        check_vma=False,
    )
```

```python
import jax
import jax.numpy as jnp
import ml_dtypes
import numpy as np
from jax import lax
from jax.experimental import pallas as pl
from jax.experimental.pallas import tpu as pltpu
from jax.sharding import PartitionSpec as P

MESH = pl.DeviceIdType.MESH
F32 = jnp.float32
BF16 = jnp.bfloat16

NP = 7
NN = 49
NZ = 512
MODES = 32
PLANES = 8
LOCAL = 16
ELEMS = 128
SPAN_WAVENUMBER = 0.25
GROUPS = 6

GLL_POINTS = (
    -1.0,
    -0.830223896278567,
    -0.468848793470714,
    0.0,
    0.468848793470714,
    0.830223896278567,
    1.0,
)

PIECES = (
    (0, 0, 0, 32),
    (3, 0, 32, 17),
    (3, 17, 81, 15),
    (1, 0, 49, 32),
    (4, 0, 130, 17),
    (4, 17, 96, 2),
    (2, 0, 98, 32),
)
TRACES = (
    (0, 0, 13, 4, 19),
    (0, 13, 15, 6, 0),
    (1, 0, 28, 5, 0),
    (2, 0, 4, 5, 28),
    (2, 4, 16, 7, 0),
    (2, 20, 8, 8, 0),
)
RETURNS = (
    tuple(range(0, 32)),
    tuple(range(49, 81)),
    tuple(range(98, 130)),
    tuple(range(32, 49)) + tuple(range(81, 96)),
)
HALF = tuple(range(130, 146))
QUARTER = (146, 96, 97)


def derivative_matrix():
    points = np.array(GLL_POINTS)
    identity = np.eye(NP)
    offdiag = points[:, None] - points[None, :] + identity
    weights = 1.0 / np.prod(offdiag, axis=1)
    matrix = weights[None, :] / weights[:, None] / offdiag
    matrix = matrix * (1.0 - identity)
    return matrix - identity * matrix.sum(axis=1)[:, None]


def split_np(table):
    table = table.astype(np.float32)
    high = table.astype(ml_dtypes.bfloat16)
    low = (table - high.astype(np.float32)).astype(ml_dtypes.bfloat16)
    return high, low


def side_node(side, position):
    return (position, position * NP + NP - 1, (NP - 1) * NP + position, position * NP)[side]


def tables():
    index = np.arange(NZ)
    wave = np.where(index == 1, NZ // 2, index // 2)
    phase = (wave[:, None] * index[None, :] % NZ) * (2.0 * np.pi / NZ)
    sine_row = ((index % 2 == 1) & (index > 1))[:, None]
    inverse = np.where(sine_row, np.sin(phase), np.cos(phase))
    slope = np.where(index < 2, 0.0, wave)[:, None] * SPAN_WAVENUMBER
    slope = slope * np.where(sine_row, np.cos(phase), -np.sin(phase))
    high, low = split_np(np.concatenate([inverse.T, slope.T], axis=0))
    backward = np.concatenate([high, low, high], axis=1)
    weighting = np.where(index < 2, 1.0, 2.0) / NZ
    high, low = split_np(inverse * weighting[:, None])
    forward = np.concatenate([high, low, high], axis=1)
    matrix = derivative_matrix()
    derive = np.zeros((256, 512))
    for j in range(NP):
        for i in range(NP):
            for b in range(NP):
                for e in range(4):
                    derive[4 * (j * NP + b) + e, 4 * (j * NP + i) + e] = matrix[i, b]
                    derive[4 * (b * NP + i) + e, 256 + 4 * (j * NP + i) + e] = matrix[j, b]
    high, low = split_np(derive)
    derive = np.concatenate([high, high, low], axis=0)
    place = np.zeros((3, 256, 512))
    starts = {(0, 0): 76, (0, 13): 128, (1, 0): 0, (2, 0): 112, (2, 4): 128, (2, 20): 192}
    for comp, first, count, _, _ in TRACES:
        for k in range(count):
            side, position = divmod(first + k, NP)
            for e in range(4):
                column = 256 * (side % 2) + 4 * side_node(side, position) + e
                place[comp, starts[comp, first] + 4 * k + e, column] = 1.0
    place = place.astype(ml_dtypes.bfloat16)
    place[1, 128:] = place[1, :128]
    return backward, forward, derive, np.concatenate([place, place], axis=1)


def halves(value):
    high = value.astype(BF16)
    return high, (value - high.astype(F32)).astype(BF16)


def lane_swap(load, store):
    lane = lax.broadcasted_iota(jnp.int32, (8, 128), 1)
    tiles = [None] * 32
    for p in range(32):
        tiles[-p % 32] = pltpu.roll(load(p), 4 * p, 1) if p else load(p)
    for bit in range(5):
        mask = (lane & (4 << bit)) != 0
        tiles = [jnp.where(mask, tiles[(j - (1 << bit)) % 32], tiles[j]) for j in range(32)]
    for d in range(32):
        store(d, pltpu.roll(tiles[d], 128 - 4 * d, 1) if d else tiles[d])


def matmul(a, b):
    return jnp.dot(a, b, preferred_element_type=F32)


def matmul_nt(a, b):
    return lax.dot_general(a, b, (((1,), (1,)), ((), ())), preferred_element_type=F32)


def exact(a, b):
    return jnp.dot(a, b, precision=lax.Precision.HIGHEST, preferred_element_type=F32)


def main_kernel(
    v_hbm,
    metric_hbm,
    lift_hbm,
    nb_hbm,
    ns_hbm,
    or_hbm,
    inv_hbm,
    fwd_hbm,
    der_hbm,
    place_hbm,
    done,
    back,
    back_h,
    back_q,
    vn,
    vs,
    vp,
    sb,
    sp,
    rx,
    rp,
    sb2,
    sh2,
    sq2,
    inv,
    fwd,
    der,
    place,
    met,
    lif,
    nbv,
    nsv,
    orv,
    lmat,
    kmat,
    oh,
    sel,
    oht,
    up_out,
    dn_out,
    up_in,
    dn_in,
    rows,
    xr,
    pv,
    dlhs,
    dxe,
    base,
    uu,
    xa,
    pa,
    la,
    xp,
    tail,
    load_sem,
    in_sem,
    send_sem,
    recv_sem,
    send2_sem,
    recv2_sem,
    halo_send,
    halo_recv,
    ready_sem,
):
    me = lax.axis_index("mode")
    part = lax.axis_index("plane")
    has_above = part < PLANES - 1
    has_below = part > 0
    above = lax.rem(part + 1, PLANES)
    below = lax.rem(part + PLANES - 1, PLANES)

    barrier = pltpu.get_barrier_semaphore()

    @pl.loop(1, MODES, unroll=True)
    def _(k):
        pl.semaphore_signal(
            barrier, inc=1, device_id={"mode": lax.rem(me + k, MODES)}, device_id_type=MESH
        )

    @pl.when(has_above)
    def _():
        pl.semaphore_signal(barrier, inc=1, device_id={"plane": above}, device_id_type=MESH)

    def entered():
        @pl.when(has_below)
        def _():
            pl.semaphore_wait(barrier, MODES)
            pl.semaphore_signal(ready_sem, inc=1, device_id={"plane": below}, device_id_type=MESH)

        @pl.when(part == 0)
        def _():
            pl.semaphore_wait(barrier, MODES - 1)

    nbv[...] = jnp.full((8, 128), -1, jnp.int32)
    nsv[...] = jnp.zeros((8, 128), jnp.int32)
    orv[...] = jnp.zeros((8, 128), jnp.int32)
    met[...] = jnp.zeros_like(met)
    lif[...] = jnp.zeros_like(lif)
    loads = []
    for k, (group, slot, row, count) in enumerate(PIECES):
        copy = pltpu.make_async_copy(
            v_hbm.at[pl.ds(row, count)], vs.at[group, pl.ds(slot, count)], load_sem.at[k]
        )
        copy.start()
        loads.append((group, copy))
    others = []
    for k, (src, dst) in enumerate(
        (
            (v_hbm, vn),
            (nb_hbm, nbv.at[pl.ds(0, 4)]),
            (ns_hbm, nsv.at[pl.ds(0, 4)]),
            (or_hbm, orv.at[pl.ds(0, 4)]),
            (metric_hbm, met.at[:, pl.ds(0, 4)]),
            (lift_hbm, lif.at[:, pl.ds(0, 4)]),
            (inv_hbm, inv),
            (der_hbm, der),
            (place_hbm, place),
            (fwd_hbm, fwd),
        )
    ):
        copy = pltpu.make_async_copy(src, dst, in_sem.at[k])
        copy.start()
        others.append(copy)

    vp[...] = jnp.zeros_like(vp)

    @pl.when(part == 0)
    def _():
        up_in[...] = jnp.zeros_like(up_in)

    @pl.when(part == PLANES - 1)
    def _():
        dn_in[...] = jnp.zeros_like(dn_in)

    def scatter(group):
        @pl.loop(0, 2)
        def _(half):
            rows8 = pl.ds(pl.multiple_of(half * 8, 8), 8)

            def store(d, tile):
                sb[group, d, rows8] = tile

            lane_swap(lambda p: vs[group, p, rows8], store)

    def send(group):
        mine = rx.at[group, pl.ds(pl.multiple_of(me * LOCAL, LOCAL), LOCAL)]
        pltpu.make_async_copy(sb.at[group, me], mine, recv_sem.at[group]).start()

        @pl.loop(1, MODES)
        def _(k):
            to = lax.rem(me + k, MODES)
            pltpu.make_async_remote_copy(
                src_ref=sb.at[group, to],
                dst_ref=mine,
                send_sem=send_sem.at[group],
                recv_sem=recv_sem.at[group],
                device_id={"mode": to},
                device_id_type=MESH,
            ).start()

    def depart(group):
        for owner, copy in loads:
            if owner == group:
                copy.wait()
        scatter(group)
        if group == 0:
            entered()
        send(group)

    def part_rows(group):
        return pl.ds(0, 4 if group == 8 else 8)

    def depart_part(group):
        k = group - GROUPS

        def store(d, tile):
            sp[k, d] = tile

        lane_swap(lambda p: vp[k, p], store)
        some = part_rows(group)
        pltpu.make_async_copy(sp.at[k, me, some], rp.at[k, me, some], recv_sem.at[group]).start()

        @pl.loop(1, MODES)
        def _(j):
            to = lax.rem(me + j, MODES)
            pltpu.make_async_remote_copy(
                src_ref=sp.at[k, to, some],
                dst_ref=rp.at[k, me, some],
                send_sem=send_sem.at[group],
                recv_sem=recv_sem.at[group],
                device_id={"mode": to},
                device_id_type=MESH,
            ).start()

    for group in (0, 3, 1):
        depart(group)

    for copy in others[:4]:
        copy.wait()
    nb = nbv[...]
    exists = nb >= 0
    owner = lax.shift_right_arithmetic(nb, 7)
    target = nsv[...] * ELEMS + (nb & (ELEMS - 1))
    own_key = jnp.where(exists & (owner == part), target, -1)
    is_up = exists & (owner == part + 1)
    is_dn = exists & (owner == part - 1)
    strict = (
        lax.broadcasted_iota(jnp.int32, (128, 128), 0)
        < lax.broadcasted_iota(jnp.int32, (128, 128), 1)
    ).astype(F32)
    ranks = []
    for border in (is_up, is_dn):
        flag = jnp.where(border, 1.0, 0.0)
        before = exact(flag, strict)
        totals = jnp.sum(flag, axis=1, keepdims=True)
        offset = jnp.zeros((1, 1), F32)
        found = []
        for side in range(4):
            found.append(before[side : side + 1] + offset)
            offset = offset + totals[side : side + 1]
        ranks.append(found)
    row128 = lax.broadcasted_iota(jnp.int32, (128, 128), 0).astype(F32)
    row512 = lax.broadcasted_iota(jnp.int32, (512, 128), 0)
    for side in range(4):
        lanes = pl.ds(side * 128, 128)
        one = slice(side, side + 1)
        slot = jnp.where(
            is_up[one], ranks[0][side], jnp.where(is_dn[one], 32.0 + ranks[1][side], -1.0)
        )
        sel[:, lanes] = jnp.where(row128 == slot, 1.0, 0.0).astype(BF16)
        oh[:, lanes] = jnp.where(row512 == own_key[one], 1.0, 0.0).astype(BF16)
        high, low = halves(jnp.broadcast_to((target[one] + 1).astype(F32), (16, 128)))
        kmat[pl.ds(0, 16), lanes] = high
        kmat[pl.ds(16, 16), lanes] = low
    turned = orv[...] == 1

    @pl.loop(0, 3)
    def _(comp):
        for position in range(NP):
            for side in range(4):
                straight = vn[comp * NN + side_node(side, position)]
                reverse = vn[comp * NN + side_node(side, NP - 1 - position)]
                value = jnp.where(turned[side : side + 1], reverse, straight)
                high, low = halves(value)
                lanes = pl.ds(side * 128, 128)
                lmat[comp, pl.ds(position * 16, 16), lanes] = high
                lmat[comp, pl.ds(112 + position * 16, 16), lanes] = low

    picked = []
    for comp in range(3):
        both = matmul_nt(lmat[comp], sel[...])
        picked.append(both[:112] + both[112:])
    both = matmul_nt(kmat[...], sel[...])
    keys = jnp.concatenate([both[:16] + both[16:], jnp.zeros((96, 128), F32)], axis=0)
    picked.append(keys)
    lane = lax.broadcasted_iota(jnp.int32, (112, 128), 1)
    for ref, shift in ((up_out, 0), (dn_out, 96)):
        packed = None
        for k in (3, 2, 1, 0):
            by = (32 * k + shift) % 128
            moved = pltpu.roll(picked[k], by, 1) if by else picked[k]
            packed = moved if packed is None else jnp.where(lane < 32 * k + 32, moved, packed)
        ref[...] = packed
    halo = [
        pltpu.make_async_remote_copy(
            src_ref=src,
            dst_ref=dst,
            send_sem=halo_send.at[k],
            recv_sem=halo_recv.at[k],
            device_id={"plane": to},
            device_id_type=MESH,
        )
        for k, (src, dst, to) in enumerate(((up_out, up_in, above), (dn_out, dn_in, below)))
    ]

    @pl.when(has_below)
    def _():
        halo[1].start()

    @pl.when(has_above)
    def _():
        pl.semaphore_wait(ready_sem, 1)
        halo[0].start()

    for copy in others[4:6]:
        copy.wait()
    fold = (
        lax.broadcasted_iota(jnp.int32, (128, 256), 0)
        == 4 * me + (lax.broadcasted_iota(jnp.int32, (128, 256), 1) & 3)
    ).astype(F32)
    spread = exact(met[...].reshape(NN * 8, 128), fold).reshape(NN, 8, 256)
    node3 = lax.shift_right_arithmetic(lax.broadcasted_iota(jnp.int32, (NN, 8, 256), 2), 2)
    here = node3 == lax.broadcasted_iota(jnp.int32, (NN, 8, 256), 0)
    metric_rows = jnp.sum(jnp.where(here, spread, 0.0), axis=0)
    rows[pl.ds(0, 4)] = metric_rows[:4]
    live = exact(jnp.where(exists, 0.5, 0.0), fold)
    spread = exact(lif[...].reshape(2 * NP * 8, 128), fold).reshape(2 * NP, 8, 256)
    node2 = lax.shift_right_arithmetic(lax.broadcasted_iota(jnp.int32, (8, 256), 1), 2)
    side2 = lax.broadcasted_iota(jnp.int32, (8, 256), 0)
    for axis in range(2):
        total = jnp.zeros((8, 256), F32)
        for position in range(NP):
            wanted = jnp.full((8, 256), -1, jnp.int32)
            for side in range(4):
                wanted = jnp.where(side2 == side, side_node(side, position), wanted)
            total = total + jnp.where(node2 == wanted, spread[axis * NP + position], 0.0)
        total = total * live
        rows[pl.ds(4 + axis, 1)] = total[0:1] + total[2:3]
        rows[pl.ds(6 + axis, 1)] = total[1:2] + total[3:4]

    @pl.when(has_below)
    def _():
        halo[0].wait_recv()

    @pl.when(has_above)
    def _():
        halo[1].wait_recv()

    lane1 = lax.broadcasted_iota(jnp.int32, (8, 128), 1)
    key_up = pltpu.roll(up_in[pl.ds(0, 8)], 32, 1)
    key_dn = pltpu.roll(dn_in[pl.ds(0, 8)], 64, 1)
    key = jnp.where(lane1 < 32, key_up, jnp.where(lane1 < 64, key_dn, 0.0))[0:1]
    oht[...] = jnp.where((row512 + 1).astype(F32) == key, 1.0, 0.0).astype(BF16)
    for comp in range(3):
        both = matmul(lmat[comp], oh[...])
        across = both[:112] + both[112:]
        from_up = pltpu.roll(up_in[...], (128 - 32 * comp) % 128, 1) if comp else up_in[...]
        from_dn = pltpu.roll(dn_in[...], (160 - 32 * comp) % 128, 1) if comp != 1 else dn_in[...]
        high, low = halves(jnp.where(lane < 32, from_up, jnp.where(lane < 64, from_dn, 0.0)))
        both = matmul_nt(jnp.concatenate([high, low], axis=0), oht[...])
        across = across + (both[:112] + both[112:])
        for owner, first, count, group, slot in TRACES:
            if owner != comp:
                continue
            for k in range(count):
                side, position = divmod(first + k, NP)
                lanes = slice(side * 128, side * 128 + 128)
                where = slice(position * 16, position * 16 + 16)
                if group < GROUPS:
                    vs[group, slot + k] = across[where, lanes]
                    continue
                parts = 4 if group == 8 else 2
                for part_at in range(parts):
                    size = 16 // parts
                    at = position * 16 + part_at * size
                    vp[group - GROUPS, part_at * (32 // parts) + k, pl.ds(0, size)] = across[
                        at : at + size, lanes
                    ]
        if comp == 0:
            depart(4)
            depart(2)
            depart_part(6)
        elif comp == 1:
            continue
        else:
            depart(5)
            depart_part(7)
            depart_part(8)

    def received(group):
        ref = rx.at[group] if group < GROUPS else rp.at[group - GROUPS, :, part_rows(group)]
        pltpu.make_async_copy(ref, ref, recv_sem.at[group]).wait()

    for copy in others[6:]:
        copy.wait()
    lane64 = lax.broadcasted_iota(jnp.int32, (64, 128), 1)

    def gather(pieces):
        @pl.loop(0, 8)
        def _(block):
            at = pl.multiple_of(block * 64, 64)
            for k in range(2):
                high, low = halves(pieces[k](pl.ds(at, 64)))
                lanes = pl.ds(k * 128, 128)
                xr[pl.ds(at, 64), lanes] = high
                xr[pl.ds(at + 512, 64), lanes] = high
                xr[pl.ds(at + 1024, 64), lanes] = low

    def derive(comp):
        @pl.loop(0, 8)
        def _(block):
            rows64 = pl.ds(pl.multiple_of(block * 64, 64), 64)
            high, low = halves(pv[comp, rows64])
            dlhs[rows64, pl.ds(0, 256)] = high
            dlhs[rows64, pl.ds(256, 256)] = low
            dlhs[rows64, pl.ds(512, 256)] = high

        dxe[comp] = matmul(dlhs[...], der[...])

    def joined(rows64):
        return jnp.where(
            lane64 < 60, pltpu.roll(rx[3, rows64], 60, 1), pltpu.roll(rx[4, rows64], 120, 1)
        )

    received(0)
    received(3)
    gather((lambda r: rx[0, r], lambda r: rx[3, r]))
    pv[0] = matmul(inv[...], xr[...])
    derive(0)
    received(1)
    received(4)
    gather((lambda r: rx[1, r], joined))
    pv[1] = matmul(inv[...], xr[...])
    derive(1)
    received(2)
    gather((lambda r: rx[2, r], lambda r: rx[4, r]))
    pv[2, pl.ds(0, 512)] = matmul(inv[pl.ds(0, 512)], xr[...])

    def bases(comps):
        @pl.loop(0, 16)
        def _(block):
            at = pl.multiple_of(block * 32, 32)
            rows32 = pl.ds(at, 32)
            u, v, w = pv[0, rows32], pv[1, rows32], pv[2, rows32]
            first = u * rows[pl.ds(0, 1)] + v * rows[pl.ds(1, 1)]
            second = u * rows[pl.ds(2, 1)] + v * rows[pl.ds(3, 1)]
            if 0 in comps:
                uu[0, rows32] = u * rows[pl.ds(4, 1)] + v * rows[pl.ds(5, 1)]
                uu[1, rows32] = u * rows[pl.ds(6, 1)] + v * rows[pl.ds(7, 1)]
            layers = uu[0, rows32] + uu[1, rows32]
            for comp in comps:
                total = first * dxe[comp, rows32, pl.ds(0, 256)]
                total = total + second * dxe[comp, rows32, pl.ds(256, 256)]
                total = total + w * pv[comp, pl.ds(at + 512, 32)]
                base[comp, rows32] = total - layers * pv[comp, rows32]

    bases((0,))

    def send_back(index, source, target):
        pltpu.make_async_copy(source(me), target, recv2_sem.at[index]).start()

        @pl.loop(1, MODES, unroll=True)
        def _(k):
            to = lax.rem(me + k, MODES)
            pltpu.make_async_remote_copy(
                src_ref=source(to),
                dst_ref=target,
                send_sem=send2_sem.at[index],
                recv_sem=recv2_sem.at[index],
                device_id={"mode": to},
                device_id_type=MESH,
            ).start()

    def whole_back(group):
        send_back(
            group,
            lambda to: sb2.at[group, pl.ds(pl.multiple_of(to * LOCAL, LOCAL), LOCAL)],
            back.at[group, me],
        )

    def traces_on_planes(slot, load):
        @pl.loop(0, 8)
        def _(block):
            at = pl.multiple_of(block * 64, 64)
            high, low = halves(load(pl.ds(at, 64)))
            xa[pl.ds(at, 64)] = high
            xa[pl.ds(at + 512, 64)] = high
            xa[pl.ds(at + 1024, 64)] = low

        pa[slot] = matmul(inv[pl.ds(0, 512)], xa[...])

    def product(comp, loads_):
        count = len(loads_)

        @pl.loop(0, 8)
        def _(block):
            rows64 = pl.ds(pl.multiple_of(block * 64, 64), 64)
            for k, load in enumerate(loads_):
                high, low = halves(load(rows64))
                la[rows64, pl.ds(128 * k, 128)] = high
                la[rows64, pl.ds(128 * (count + k), 128)] = low

        wide = pl.ds(0, 256 * count)
        dxe[0] = matmul(la[:, wide], place[comp, wide])

        @pl.loop(0, 8)
        def _(block):
            at = pl.multiple_of(block * 64, 64)
            rows64 = pl.ds(at, 64)
            total = base[comp, rows64] + uu[0, rows64] * dxe[0, rows64, pl.ds(0, 256)]
            total = total + uu[1, rows64] * dxe[0, rows64, pl.ds(256, 256)]
            high, low = halves(total)
            xp[rows64] = high
            xp[pl.ds(at + 512, 64)] = high
            xp[pl.ds(at + 1024, 64)] = low

        result = matmul(fwd[...], xp[...])
        sb2[comp] = result[:, :128]
        tail[comp] = result[:, 128:]
        whole_back(comp)

    def half_tiles(k):
        tiles = rp[k][:, None]
        return jnp.concatenate([tiles, pltpu.roll(tiles, 64, 3)], axis=1).reshape(NZ, 128)

    received(6)
    rx[6] = half_tiles(0)
    traces_on_planes(0, lambda r: rx[6, r])
    product(0, (lambda r: pv[2, r, pl.ds(128, 128)], lambda r: pa[0, r]))
    bases((1,))
    received(5)
    traces_on_planes(1, lambda r: rx[5, r])
    product(1, (lambda r: pa[1, r],))
    lane512 = lax.broadcasted_iota(jnp.int32, (512, 128), 1)
    sb2[3] = jnp.where(lane512 < 68, tail[0], pltpu.roll(tail[1], 68, 1))
    whole_back(3)
    pv[2, pl.ds(512, 512)] = matmul(inv[pl.ds(512, 512)], xr[...])
    derive(2)
    bases((2,))
    received(7)
    received(8)
    low_rows = lax.broadcasted_iota(jnp.int32, (MODES, 8, 128), 1) < 4
    tiles = rp[2]
    pairs = []
    for even, odd in ((64, 32), (0, 96)):
        upper = pltpu.roll(pltpu.roll(tiles, odd, 2), 4, 1)
        lower = pltpu.roll(tiles, even, 2) if even else tiles
        pairs.append(jnp.where(low_rows, lower, upper)[:, None])
    quarter = jnp.concatenate(pairs, axis=1).reshape(NZ, 128)
    rx[6] = jnp.where(lane512 < 64, half_tiles(1), jnp.where(lane512 < 96, quarter, 0.0))
    traces_on_planes(0, lambda r: rx[6, r])
    product(2, (lambda r: pa[1, r], lambda r: pa[0, r]))
    lane3 = lax.broadcasted_iota(jnp.int32, (MODES, 8, 128), 2)
    ends = tail[2].reshape(MODES, 2, 8, 128)
    sh2[...] = jnp.where(lane3 < 64, ends[:, 0], pltpu.roll(ends[:, 1], 64, 2))
    send_back(4, lambda to: sh2.at[to], back_h.at[me])

    others1 = tail[1].reshape(MODES, 2, 8, 128)
    packed = None
    for k in (1, 0):
        end = jnp.where(lane3 < 4, pltpu.roll(ends[:, k], 64, 2), pltpu.roll(others1[:, k], 72, 2))
        for upper in (1, 0):
            block = 2 * k + upper
            moved = pltpu.roll(end, 4, 1) if upper else end
            moved = pltpu.roll(moved, 32 * block, 2) if block else moved
            packed = moved if packed is None else jnp.where(lane3 < 32 * block + 32, moved, packed)
    sq2[...] = packed
    few = pl.ds(0, 4)
    send_back(5, lambda to: sq2.at[to, few], back_q.at[me, few])

    def arrived(index, ref):
        pltpu.make_async_copy(ref, ref, recv2_sem.at[index]).wait()

    for group in (0, 1, 3, 2):
        arrived(group, back.at[group])

        @pl.loop(0, 2)
        def _(half):
            rows8 = pl.ds(pl.multiple_of(half * 8, 8), 8)

            def store(d, tile):
                done[RETURNS[group][d], rows8] = tile

            lane_swap(lambda p: back[group, p, rows8], store)

    def store_half(d, tile):
        done[HALF[d % 16], pl.ds(d // 16 * 8, 8)] = tile

    arrived(4, back_h)
    lane_swap(lambda p: back_h[p], store_half)

    def store_last(d, tile):
        if d % 8 < len(QUARTER):
            done[QUARTER[d % 8], pl.ds(d // 8 * 4, 4)] = tile[:4]

    arrived(5, back_q.at[:, few])
    lane_swap(lambda p: back_q[p], store_last)

    @pl.when(has_above)
    def _():
        halo[0].wait_send()

    @pl.when(has_below)
    def _():
        halo[1].wait_send()

    for group in range(GROUPS):
        sent = sb.at[group, pl.ds(0, MODES - 1)]
        pltpu.make_async_copy(sent, sent, send_sem.at[group]).wait()
    for k in range(3):
        sent = sp.at[k, pl.ds(0, MODES - 1), part_rows(GROUPS + k)]
        pltpu.make_async_copy(sent, sent, send_sem.at[GROUPS + k]).wait()
    for group in range(4):
        sent = sb2.at[group, pl.ds(0, (MODES - 1) * LOCAL)]
        pltpu.make_async_copy(sent, sent, send2_sem.at[group]).wait()
    sent = sh2.at[pl.ds(0, MODES - 1)]
    pltpu.make_async_copy(sent, sent, send2_sem.at[4]).wait()
    sent = sq2.at[pl.ds(0, MODES - 1), few]
    pltpu.make_async_copy(sent, sent, send2_sem.at[5]).wait()


def shards(velocity, metric_terms, lift_scale, neighbour, neighbour_side, orientation):
    v = jnp.transpose(velocity, (0, 2, 1, 3)).reshape(3 * NN, LOCAL, ELEMS)
    metric = jnp.transpose(metric_terms, (1, 0, 2))
    lift = jnp.transpose(lift_scale, (0, 2, 1, 3)).reshape(2 * NP, 4, ELEMS)
    operands = [v, metric, lift, neighbour, neighbour_side, orientation]
    operands += [jnp.asarray(t) for t in tables()]
    anywhere = pl.BlockSpec(memory_space=pl.ANY)
    vmem = pltpu.VMEM
    dma = pltpu.SemaphoreType.DMA
    out = pl.pallas_call(
        main_kernel,
        out_shape=pltpu.VMEM((3 * NN, LOCAL, ELEMS), F32),
        in_specs=[anywhere] * 10,
        out_specs=pl.BlockSpec(memory_space=vmem),
        scratch_shapes=[
            vmem((4, MODES, LOCAL, 128), F32),
            vmem((MODES, 8, 128), F32),
            vmem((MODES, 8, 128), F32),
            vmem((3 * NN, LOCAL, 128), F32),
            vmem((GROUPS, 32, LOCAL, 128), F32),
            vmem((3, 32, 8, 128), F32),
            vmem((GROUPS, MODES, LOCAL, 128), F32),
            vmem((3, MODES, 8, 128), F32),
            vmem((GROUPS + 1, NZ, 128), F32),
            vmem((3, MODES, 8, 128), F32),
            vmem((4, NZ, 128), F32),
            vmem((MODES, 8, 128), F32),
            vmem((MODES, 8, 128), F32),
            vmem((2 * NZ, 3 * NZ), BF16),
            vmem((NZ, 3 * NZ), BF16),
            vmem((768, 512), BF16),
            vmem((3, 512, 512), BF16),
            vmem((NN, 8, 128), F32),
            vmem((2 * NP, 8, 128), F32),
            vmem((8, 128), jnp.int32),
            vmem((8, 128), jnp.int32),
            vmem((8, 128), jnp.int32),
            vmem((3, 224, 512), BF16),
            vmem((32, 512), BF16),
            vmem((512, 512), BF16),
            vmem((128, 512), BF16),
            vmem((512, 128), BF16),
            vmem((112, 128), F32),
            vmem((112, 128), F32),
            vmem((112, 128), F32),
            vmem((112, 128), F32),
            vmem((8, 256), F32),
            vmem((3 * NZ, 256), BF16),
            vmem((3, 2 * NZ, 256), F32),
            vmem((NZ, 768), BF16),
            vmem((3, NZ, 512), F32),
            vmem((3, NZ, 256), F32),
            vmem((2, NZ, 256), F32),
            vmem((3 * NZ, 128), BF16),
            vmem((2, NZ, 128), F32),
            vmem((NZ, 512), BF16),
            vmem((3 * NZ, 256), BF16),
            vmem((3, NZ, 128), F32),
            dma((len(PIECES),)),
            dma((10,)),
            dma((GROUPS + 3,)),
            dma((GROUPS + 3,)),
            dma((6,)),
            dma((6,)),
            dma((2,)),
            dma((2,)),
            pltpu.SemaphoreType.REGULAR,
        ],
        compiler_params=pltpu.CompilerParams(
            collective_id=0, has_side_effects=True, vmem_limit_bytes=48 << 20
        ),
        name="advect",
    )(*[pltpu.with_memory_space_constraint(x, pltpu.HBM) for x in operands])
    out = out.reshape(3, NN, LOCAL, ELEMS)
    return jnp.transpose(out, (0, 2, 1, 3))


def solution(mesh):
    return jax.shard_map(
        shards,
        mesh=mesh,
        in_specs=(
            P(None, "mode", None, "plane"),
            P(None, None, "plane"),
            P(None, None, None, "plane"),
            P(None, "plane"),
            P(None, "plane"),
            P(None, "plane"),
        ),
        out_specs=P(None, "mode", None, "plane"),
        check_vma=False,
    )
```
